32 devices in a mesh: lon: 4 (over z), lat: 2 (over core), mem: 4 (over y, x).
Axes of the slice: x: 2, y: 2, z: 4, core: 2. Of those that a mesh axis runs over, the one named last changes fastest.
Arguments:
- controls: float32 [16, 96, 48, 128], P('mem', 'lon', 'lat'), may hold values from -6 to 6
- ensemble: bfloat16 [16, 96, 48, 128], P('mem', 'lon', 'lat'), may hold values from -1.5 to 1.5
- taps_lon: float32 [17], replicated, may hold values from 0.05 to 0.35
- taps_lat: float32 [17], replicated, may hold values from 0.05 to 0.35
- obs_columns: int32 [4, 2, 4, 16], P('lon', 'lat', 'mem'), may hold values from 0 to 575
- obs_count: int32 [4, 2, 4], P('lon', 'lat', 'mem'), may hold values from 1 to 16, as said below
- obs_quality: int32 [4, 2, 4, 16], P('lon', 'lat', 'mem'), may hold values from 0 to 3
- obs_values: float32 [4, 2, 4, 16, 128], P('lon', 'lat', 'mem'), may hold values from -6 to 6
Outputs:
- new_controls: float32 [16, 96, 48, 128], P('mem', 'lon', 'lat')
- residual: float32 [4, 2, 4, 16, 128], P('lon', 'lat', 'mem')
The draws below stay inside these ranges and needn't reach their ends.
Inputs may be any that keep to these rules, and one draw needn't show every extreme that they name: `obs_columns`: column within the owner's tile, numbered as longitude offset times 24 plus latitude offset. `obs_count`: slots from this number on are unused; some owner has exactly 16 live slots.
All inputs are finite; a program needn't handle non-finite values.
Results may differ from the reference program's by a relative error of at most 0.0049.
Values may be sent and summed in bfloat16 or wider, within the bound.
No kernel may reach another device: no remote copies, remote signals or barrier semaphores. Data moves between devices by JAX's collectives and lax.ppermute only.
A program may use at most 64 MiB of HBM per device.

```python
import jax
import jax.numpy as jnp
from jax import lax

LONX = 24
LATY = 24
LEV = 128
NOBS = 16
TAPS = 17
MEMBERS = 16
NLON = 96
NLAT = 48
TILES_LON = 4
TILES_LAT = 2
OWNERS = 4


def draw_obs_count(key, part):
    first, second = jax.random.split(key)
    choose = jax.random.randint(first, (TILES_LON, TILES_LAT, OWNERS), 0, 4)
    light = jax.random.randint(second, (TILES_LON, TILES_LAT, OWNERS), 1, NOBS // 4 + 1)
    counts = jnp.where(choose == 0, NOBS, light)
    return counts.at[0, 0, 0].set(NOBS).astype(jnp.int32)


def plant(values, own_key, least, high):
    place = [jax.random.randint(jax.random.fold_in(own_key, axis), (), 0, length) for axis, length in enumerate(values.shape)]
    widest = values.shape.index(max(values.shape))
    next_to = place[:widest] + [(place[widest] + 1) % values.shape[widest]] + place[widest + 1:]
    return values.at[tuple(place)].set(least).at[tuple(next_to)].set(high)


def level_of(key, shape, cuts, smallest, top_value):
    factor_of, own = 1.0, jax.random.fold_in(key, 6)
    for dim, blocks in cuts:
        draws = jnp.exp(jax.random.uniform(jax.random.fold_in(own, dim), (blocks,), jnp.float32, smallest / len(cuts), top_value / len(cuts)))
        factor_of = factor_of * jnp.repeat(draws, shape[dim] // blocks).reshape([-1 if axis == dim else 1 for axis in range(len(shape))])
    return factor_of


def scatter_about(own_key, shape, width, limit, shards=(), dtype=jnp.bfloat16):
    entries = jax.random.normal(own_key, shape, jnp.float32) * width
    if len(shards) > 0:
        entries = level_of(own_key, shape, shards, -0.22, 0.18) * entries
    return jnp.clip(entries, min=-limit, max=limit).astype(dtype)


def setup_inputs(seed: int = 0) -> dict:
    splits = jax.random.split(jax.random.key(seed), 9)
    return {
        "controls": scatter_about(splits[0], (MEMBERS, NLON, NLAT, LEV), 1.0, 6.0, ((0, 4), (1, 4), (2, 2)), jnp.float32),
        "ensemble": scatter_about(splits[1], (MEMBERS, NLON, NLAT, LEV), 0.25, 1.5, ((0, 4), (1, 4), (2, 2))),
        "taps_lon": jnp.clip(jax.random.uniform(splits[2], (TAPS,), jnp.float32, 0.05, 0.35), 0.05, 0.35),
        "taps_lat": jnp.clip(jax.random.uniform(splits[3], (TAPS,), jnp.float32, 0.05, 0.35), 0.05, 0.35),
        "obs_columns": plant(jax.random.randint(splits[4], (TILES_LON, TILES_LAT, OWNERS, NOBS), 0, LONX * LATY), jax.random.fold_in(splits[4], 1), 0, (LONX * LATY) - 1).astype(jnp.int32),
        "obs_count": draw_obs_count(jax.random.fold_in(splits[8], 71), 0),
        "obs_quality": plant(jax.random.randint(splits[6], (TILES_LON, TILES_LAT, OWNERS, NOBS), 0, 4), jax.random.fold_in(splits[6], 1), 0, 3).astype(jnp.int32),
        "obs_values": scatter_about(splits[7], (TILES_LON, TILES_LAT, OWNERS, NOBS, LEV), 1.0, 6.0, ((0, 4), (1, 2), (2, 4)), jnp.float32),
    }


descent = 0.5


def rounded(value):
    return lax.optimization_barrier(value.astype(jnp.bfloat16)).astype(jnp.float32)


def lon_conv(field, kernel):
    tap_count = kernel.shape[0]
    rim_width = tap_count // 2
    result = jnp.zeros_like(field)
    for tap_index in range(tap_count):
        result = result + kernel[tap_index] * jnp.roll(field, rim_width - tap_index, axis=0)
    return result


def lat_conv(field, kernel):
    tap_count = kernel.shape[0]
    rim_width = tap_count // 2
    width_lat = field.shape[1]
    padded = jnp.pad(field, ((0, 0), (rim_width, rim_width), (0, 0)))
    result = jnp.zeros_like(field)
    for tap_index in range(tap_count):
        result = result + kernel[tap_index] * padded[:, tap_index:tap_index + width_lat]
    return result


def pick_rows(tile_grid, picked):
    return tile_grid[picked]


def spread_back(values, picked):
    return jnp.zeros((LONX * LATY, LEV), jnp.float32).at[picked].add(values)


def reference(controls, ensemble, taps_lon, taps_lat, obs_columns, obs_count, obs_quality, obs_values):
    kernel_lon = rounded(taps_lon)
    kernel_lat = rounded(taps_lat)

    def accumulate(total, pair):
        control, member = pair
        spread = lat_conv(rounded(lon_conv(rounded(control), kernel_lon)), kernel_lat)
        return total + member.astype(jnp.float32) * spread, None

    increment, _ = lax.scan(accumulate, jnp.zeros((NLON, NLAT, LEV), jnp.float32), (controls, ensemble))
    tiled = increment.reshape(TILES_LON, LONX, TILES_LAT, LATY, LEV).transpose(0, 2, 1, 3, 4)
    tiled = tiled.reshape(TILES_LON * TILES_LAT, LONX * LATY, LEV)
    columns = obs_columns.reshape(TILES_LON * TILES_LAT, OWNERS * NOBS)
    observed = jax.vmap(pick_rows)(tiled, columns).reshape(TILES_LON, TILES_LAT, OWNERS, NOBS, LEV)
    active = jnp.arange(NOBS)[None, None, None, :] < obs_count[..., None]
    weights = jnp.where(active, 0.5 * obs_quality.astype(jnp.float32), jnp.zeros((), jnp.float32))
    residual = weights[..., None] * (observed - obs_values)
    adjoint_tiles = jax.vmap(spread_back)(residual.reshape(TILES_LON * TILES_LAT, OWNERS * NOBS, LEV), columns)
    adjoint = adjoint_tiles.reshape(TILES_LON, TILES_LAT, LONX, LATY, LEV).transpose(0, 2, 1, 3, 4)
    adjoint = adjoint.reshape(NLON, NLAT, LEV)
    flip_lon = kernel_lon[::-1]
    flip_lat = kernel_lat[::-1]

    def update(pair):
        control, member = pair
        product = rounded(member.astype(jnp.float32) * adjoint)
        lon_back = lon_conv(rounded(lat_conv(product, flip_lat)), flip_lon)
        return control - descent * (control + lon_back)

    new_controls = lax.map(update, (controls, ensemble))
    return new_controls, residual
```

```python
import functools

import jax
import jax.numpy as jnp
from jax import lax
from jax.experimental import pallas as pl
from jax.experimental.pallas import tpu as pltpu
from jax.sharding import PartitionSpec as P

descent = 0.5
f32 = jnp.float32
bf16 = jnp.bfloat16


def pairings(size, wraps):
    even = [(i, i ^ 1) for i in range(size)]
    odd = []
    for i in range(size):
        j = i + 1 if i % 2 else i - 1
        if wraps:
            j = j % size
        if 0 <= j < size:
            odd.append((i, j))
    return [even, odd] if odd else [even]


def band(distance, taps_ref):
    out = jnp.zeros_like(distance)
    for k in range(taps_ref.shape[0]):
        out = jnp.where(distance == float(k), taps_ref[k], out)
    return out


def fiota(shape, dim):
    return lax.broadcasted_iota(jnp.int32, shape, dim).astype(f32)


def dot(a, b):
    return jnp.dot(a, b, preferred_element_type=f32)


def obs_by_cell(lon_pos, lat_pos, taps_lon, taps_lat, lon_count, lat_count, start):
    slots, rim = lon_pos.shape[0], taps_lon.shape[0] // 2
    wide = 128
    lon_w = band(fiota((slots, wide), 1) + (start + rim) - lon_pos, taps_lon)
    lat_w = band(fiota((slots, wide), 1) + rim - lat_pos, taps_lat)
    cells = lon_count * lat_count
    cell = fiota((wide, cells), 1)
    lon_of = jnp.zeros((wide, cells), f32)
    for t in range(1, lon_count):
        lon_of = lon_of + (cell >= float(t * lat_count)).astype(f32)
    lat_of = cell - lon_of * float(lat_count)
    place = fiota((wide, cells), 0)
    lon_e = dot(lon_w.astype(bf16), (place == lon_of).astype(bf16))
    lat_e = dot(lat_w.astype(bf16), (place == lat_of).astype(bf16))
    return (lon_e * lat_e).astype(bf16)


def cell_by_obs(lon_pos, lat_pos, taps_lon, taps_lat, lon_count, lat_count, start):
    slots, rim = lon_pos.shape[1], taps_lon.shape[0] // 2
    tall = 32
    lon_w = band(fiota((tall, slots), 0) + (start + rim) - lon_pos, taps_lon)
    lat_w = band(fiota((tall, slots), 0) + rim - lat_pos, taps_lat)
    cells = lon_count * lat_count
    lon_of = fiota((lon_count, lat_count, tall), 0).reshape(cells, tall)
    lat_of = fiota((lon_count, lat_count, tall), 1).reshape(cells, tall)
    place = fiota((cells, tall), 1)
    lon_e = dot((place == lon_of).astype(bf16), lon_w.astype(bf16))
    lat_e = dot((place == lat_of).astype(bf16), lat_w.astype(bf16))
    return (lon_e * lat_e).astype(bf16)


def pick_kernel(lat_tile, info_ref, ens_ref, out_ref):
    members, cells, levels = ens_ref.shape
    slots = info_ref.shape[0]
    cell_of = info_ref[:, 0:1] * float(lat_tile) + info_ref[:, 1:2]
    chosen = (fiota((slots, cells), 1) == cell_of).astype(bf16)
    for m in range(members):
        out_ref[:, m * levels:(m + 1) * levels] = dot(chosen, ens_ref[m]).astype(bf16)
    out_ref[:, members * levels:] = info_ref[...].astype(bf16)


def prep_kernel(dims, nbrs, *refs):
    lon_tile, lat_tile, rim = dims
    taps_lon, taps_lat, off_ref, con_ref = refs[:4]
    sets = refs[4:5 + nbrs]
    base_ref, rim1_ref, rim2_ref, turned_ref = refs[5 + nbrs:]
    members, cells, levels = con_ref.shape
    slots = sets[0].shape[0]
    at = members * levels
    for s in range(1 + nbrs):
        lon_pos = sets[s][:, at:at + 128].astype(f32)[:, 0:1]
        lat_pos = sets[s][:, at:at + 128].astype(f32)[:, 1:2]
        if s == 0:
            square = (slots, slots)
            same = lax.broadcasted_iota(jnp.int32, square, 0) == lax.broadcasted_iota(jnp.int32, square, 1)
            turned_ref[...] = jnp.zeros_like(turned_ref)
            turned_ref[0:1, 0:slots] = jnp.sum(jnp.where(same, lon_pos, 0.0), axis=0, keepdims=True)
            turned_ref[1:2, 0:slots] = jnp.sum(jnp.where(same, lat_pos, 0.0), axis=0, keepdims=True)
        else:
            lat_pos = lat_pos + off_ref[1 + s]
        rows = slice(s * slots, (s + 1) * slots)
        weight = obs_by_cell(lon_pos, lat_pos, taps_lon, taps_lat, lon_tile, lat_tile, 0.0)
        for m in range(members):
            base_ref[rows, m * levels:(m + 1) * levels] = dot(weight, con_ref[m].astype(bf16))
        for ref, off in ((rim1_ref, off_ref[0]), (rim2_ref, off_ref[1])):
            ref[rows, :] = obs_by_cell(lon_pos, lat_pos, taps_lon, taps_lat, rim, lat_tile, off)


def part_kernel(nbrs, *refs):
    base_ref, w1_ref, w2_ref, h1_ref, h2_ref = refs[:5]
    sets = refs[5:6 + nbrs]
    outs = refs[6 + nbrs:]
    members, _, levels = h1_ref.shape
    slots = sets[0].shape[0]
    total = [jnp.zeros((slots, levels), f32) for _ in sets]
    for m in range(members):
        lanes = slice(m * levels, (m + 1) * levels)
        spread = base_ref[:, lanes] + dot(w1_ref[...], h1_ref[m]) + dot(w2_ref[...], h2_ref[m])
        for s in range(1 + nbrs):
            total[s] += spread[s * slots:(s + 1) * slots] * sets[s][:, lanes].astype(f32)
    for s in range(1 + nbrs):
        outs[s][...] = total[s]


def resid_kernel(a_ref, b_ref, meta_ref, own_ref, turned_ref, resid_ref, send_ref):
    slots, levels = a_ref.shape
    wide = send_ref.shape[1]
    weight = meta_ref[:, levels + 2:levels + 3]
    resid = weight * (a_ref[...] + b_ref[...] - meta_ref[:, :levels])
    resid_ref[...] = resid
    for m in range(wide // levels):
        lanes = slice(m * levels, (m + 1) * levels)
        send_ref[0:slots, lanes] = (own_ref[:, lanes].astype(f32) * resid).astype(bf16)
    send_ref[slots:, :] = turned_ref[...].astype(bf16)


def back_kernel(dims, count, taps_lon, taps_lat, off_ref, con_ref, *refs):
    lon_tile, lat_tile, lon_step = dims
    sets, out_ref, all_ref = refs[:count], refs[count], refs[count + 1]
    members, block, levels = con_ref.shape
    slots = sets[0].shape[0] - 16
    step = pl.program_id(0)
    lon_pos, lat_pos = [], []
    for s in range(count):
        tail = sets[s][slots:, 0:slots].astype(f32)
        lon_pos.append(tail[0:1] + off_ref[2 * s])
        lat_pos.append(tail[1:2] + off_ref[2 * s + 1])

    @pl.when(step == 0)
    def _():
        for s in range(count):
            all_ref[s * slots:(s + 1) * slots, :] = sets[s][0:slots, :]

    weight = cell_by_obs(
        jnp.concatenate(lon_pos, axis=1), jnp.concatenate(lat_pos, axis=1), taps_lon, taps_lat, lon_step, lat_tile,
        (step * lon_step).astype(f32),
    )
    back = dot(weight, all_ref[...])
    for m in range(members):
        con = con_ref[m]
        out_ref[m] = con - descent * (con + back[:, m * levels:(m + 1) * levels])


def shards(controls, ensemble, taps_lon, taps_lat, obs_columns, obs_count, obs_quality, obs_values):
    rim = taps_lon.shape[0] // 2
    members, lon_tile, lat_tile, levels = controls.shape
    n_slots = obs_columns.shape[-1]
    n_mem = lax.axis_size("mem")
    slots = n_slots * n_mem
    cells = lon_tile * lat_tile
    wide = members * levels
    lon_pairs = pairings(lax.axis_size("lon"), True)
    lat_pairs = pairings(lax.axis_size("lat"), False)
    nbrs = len(lat_pairs)
    mem_bits = [b for b in range(n_mem.bit_length() - 1)]
    lon_even = lax.axis_index("lon") % 2 == 0
    lat_even = lax.axis_index("lat") % 2 == 0
    mem = lax.axis_index("mem")
    vmem = pl.BlockSpec(memory_space=pltpu.VMEM)
    smem = pl.BlockSpec(memory_space=pltpu.SMEM)
    params = pltpu.CompilerParams(vmem_limit_bytes=32 * 1024 * 1024)

    taps_lon = taps_lon.astype(bf16).astype(f32)
    taps_lat = taps_lat.astype(bf16).astype(f32)

    starts = [jnp.where(lon_even, lon_tile - rim, 0), jnp.where(lon_even, 0, lon_tile - rim)]
    rims = [lax.dynamic_slice_in_dim(controls, s, rim, axis=1).astype(bf16).reshape(members, rim * lat_tile, levels) for s in starts]
    halos = [lax.ppermute(r, "lon", p) for r, p in zip(rims, lon_pairs)]
    lon_sign = [jnp.where(lon_even, 1.0, -1.0), jnp.where(lon_even, -1.0, 1.0)]
    lat_sign = [jnp.where(lat_even, 1.0, -1.0), jnp.where(lat_even, -1.0, 1.0)][:nbrs]

    active = jnp.arange(n_slots) < obs_count[0, 0, 0]
    weights = jnp.where(active, 0.5 * obs_quality[0, 0, 0].astype(f32), 0.0)
    columns = obs_columns[0, 0, 0]
    info = jnp.stack([(columns // lat_tile).astype(f32), (columns % lat_tile).astype(f32), weights], axis=1)
    meta = jnp.concatenate([obs_values[0, 0, 0], jnp.pad(info, ((0, 0), (0, 128 - 3)))], axis=1)
    for b in mem_bits:
        other = lax.ppermute(meta, "mem", [(i, i ^ (1 << b)) for i in range(n_mem)])
        upper = (mem >> b) % 2 == 1
        meta = jnp.concatenate([jnp.where(upper, other, meta), jnp.where(upper, meta, other)], axis=0)

    own = pl.pallas_call(
        functools.partial(pick_kernel, lat_tile),
        out_shape=jax.ShapeDtypeStruct((slots, wide + 128), bf16),
        in_specs=[vmem] * 2, out_specs=vmem, compiler_params=params,
    )(meta[:, levels:], ensemble.reshape(members, cells, levels))
    sets = [own] + [lax.ppermute(own, "lat", p) for p in lat_pairs]

    rim_off = [jnp.where(s > 0, float(lon_tile), float(-rim)) for s in lon_sign]
    offs = jnp.stack(rim_off + [s * lat_tile for s in lat_sign])
    total = slots * (1 + nbrs)
    base, w1, w2, turned = pl.pallas_call(
        functools.partial(prep_kernel, (lon_tile, lat_tile, rim), nbrs),
        out_shape=[
            jax.ShapeDtypeStruct((total, wide), f32),
            jax.ShapeDtypeStruct((total, rim * lat_tile), bf16),
            jax.ShapeDtypeStruct((total, rim * lat_tile), bf16),
            jax.ShapeDtypeStruct((16, wide), f32),
        ],
        in_specs=[smem] * 3 + [vmem] * (2 + nbrs), out_specs=[vmem] * 4, compiler_params=params,
    )(taps_lon, taps_lat, offs, controls.reshape(members, cells, levels), *sets)

    parts = pl.pallas_call(
        functools.partial(part_kernel, nbrs),
        out_shape=[jax.ShapeDtypeStruct((slots, levels), f32)] * (1 + nbrs),
        in_specs=[vmem] * (6 + nbrs), out_specs=[vmem] * (1 + nbrs), compiler_params=params,
    )(base, w1, w2, halos[0], halos[1], *sets)
    mine = parts[0]
    for p, q in zip(parts[1:], lat_pairs):
        mine = mine + lax.ppermute(p, "lat", q)
    for b in mem_bits:
        other = lax.ppermute(mine, "mem", [(i, i ^ (1 << b)) for i in range(n_mem)])
        if b + 1 < len(mem_bits):
            mine = mine + other

    resid, send = pl.pallas_call(
        resid_kernel,
        out_shape=[jax.ShapeDtypeStruct((slots, levels), f32), jax.ShapeDtypeStruct((slots + 16, wide), bf16)],
        in_specs=[vmem] * 5, out_specs=[vmem] * 2, compiler_params=params,
    )(mine, other, meta, own, turned)

    row = [send] + [lax.ppermute(send, "lon", p) for p in lon_pairs]
    row_off = [jnp.zeros(())] + [s * lon_tile for s in lon_sign]
    around = list(row)
    around_off = []
    for o in row_off:
        around_off += [o, jnp.zeros(())]
    for q, s in zip(lat_pairs, lat_sign):
        for r, o in zip(row, row_off):
            around.append(lax.ppermute(r, "lat", q))
            around_off += [o, s * lat_tile]
    count = len(around)
    lon_step = 8
    blocks = lon_tile // lon_step
    spec = pl.BlockSpec((members, lon_step * lat_tile, levels), lambda i: (0, i, 0))
    whole = pl.BlockSpec((slots + 16, wide), lambda i: (0, 0))
    new = pl.pallas_call(
        functools.partial(back_kernel, (lon_tile, lat_tile, lon_step), count),
        grid=(blocks,),
        out_shape=jax.ShapeDtypeStruct((members, cells, levels), f32),
        in_specs=[smem] * 3 + [spec] + [whole] * count, out_specs=spec,
        scratch_shapes=[pltpu.VMEM((count * slots, wide), bf16)],
        compiler_params=params,
    )(taps_lon, taps_lat, jnp.stack(around_off).astype(f32), controls.reshape(members, cells, levels), *around)
    mine = lax.dynamic_slice_in_dim(resid, mem * n_slots, n_slots, axis=0)
    return (new.reshape(controls.shape), mine[None, None, None])


def solution(mesh):
    placed = (
        P("mem", "lon", "lat", None),
        P("mem", "lon", "lat", None),
        P(),
        P(),
        P("lon", "lat", "mem", None),
        P("lon", "lat", "mem"),
        P("lon", "lat", "mem", None),
        P("lon", "lat", "mem", None, None),
    )
    return jax.shard_map(
        shards,
        mesh=mesh,
        in_specs=placed,
        out_specs=(P("mem", "lon", "lat", None), P("lon", "lat", "mem", None, None)),
        check_vma=False,
    )
```

```python
import functools

import jax
import jax.numpy as jnp
from jax import lax
from jax.experimental import pallas as pl
from jax.experimental.pallas import tpu as pltpu
from jax.sharding import PartitionSpec as P

descent = 0.5
f32 = jnp.float32
bf16 = jnp.bfloat16
tail = 16


def pairings(size, wraps):
    even = [(i, i ^ 1) for i in range(size)]
    odd = []
    for i in range(size):
        j = i + 1 if i % 2 else i - 1
        if wraps:
            j = j % size
        if 0 <= j < size:
            odd.append((i, j))
    return [even, odd] if odd else [even]


def sum_terms(x, count, direct=4):
    if count <= direct:
        return [x] + [lax.ppermute(x, "mem", [(i, i ^ b) for i in range(count)]) for b in range(count - 1, 0, -1)]
    step = 1
    while step < count:
        other = lax.ppermute(x, "mem", [(i, i ^ step) for i in range(count)])
        step *= 2
        if step < count:
            x = x + other
    return [x, other]


def up8(n):
    return (n + 7) // 8 * 8


def signs(axis):
    even = lax.axis_index(axis) % 2 == 0
    return [jnp.where(even, 1.0, -1.0).astype(f32), jnp.where(even, -1.0, 1.0).astype(f32)]


def fiota(shape, dim):
    return lax.broadcasted_iota(jnp.int32, shape, dim).astype(f32)


def diagonal(rows, lanes, shift=0.0):
    return fiota((rows, lanes), 0) + shift == fiota((rows, lanes), 1)


def to_rows(lanes):
    n = lanes.shape[1]
    return jnp.sum(jnp.where(diagonal(n, n), lanes, 0.0), axis=1, keepdims=True)


def to_lanes(rows):
    n = rows.shape[0]
    return jnp.sum(jnp.where(diagonal(n, n), rows, 0.0), axis=0, keepdims=True)


def lane_row(ref, first, blocks, slots):
    if blocks == 1:
        return ref[first:first + 1, 0:slots]
    return jnp.concatenate([ref[first + r:first + r + 1, :] for r in range(blocks)], axis=1)[:, 0:slots]


def band(distance, taps_ref):
    out = jnp.zeros_like(distance)
    for k in range(taps_ref.shape[0]):
        out = jnp.where(distance == float(k), taps_ref[k], out)
    return out


def dot(a, b):
    return jnp.dot(a, b, preferred_element_type=f32)


def params(mib=32):
    return pltpu.CompilerParams(vmem_limit_bytes=mib * 1024 * 1024)


def start_kernel(dims, con_ref, raw_ref, low_ref, rim1_ref, rim2_ref, info_ref):
    edge, lat_tile, n_slots, blocks = dims
    members, cells, levels = con_ref.shape
    mem = lax.axis_index("mem")
    column, quality = raw_ref[:, 0:n_slots], raw_ref[:, n_slots:2 * n_slots]
    count = raw_ref[:, 2 * n_slots:2 * n_slots + 1]
    lon_pos = jnp.floor((column + 0.5) * (1.0 / lat_tile))
    lat_pos = column - lon_pos * float(lat_tile)
    weight = jnp.where(fiota((1, n_slots), 1) < count, 0.5 * quality, 0.0)
    info_ref[...] = jnp.zeros_like(info_ref)
    row = lax.broadcasted_iota(jnp.int32, (tail, levels), 0)
    placed = jnp.zeros((tail, levels), f32)
    for f, lanes in enumerate((lon_pos, lat_pos, weight)):
        rows = to_rows(lanes)
        for r in range(blocks):
            here = diagonal(n_slots, levels, (mem * n_slots - r * levels).astype(f32))
            moved = jnp.sum(jnp.where(here, rows, 0.0), axis=0, keepdims=True)
            info_ref[f * blocks + r:f * blocks + r + 1, :] = moved
            if f < 2:
                placed = jnp.where(row == f * blocks + r, moved, placed)
    placed = placed.astype(bf16)
    even = lax.axis_index("lon") % 2 == 0
    far = cells - edge
    for at, ref in ((jnp.where(even, far, 0), rim1_ref), (jnp.where(even, 0, far), rim2_ref)):
        for m in range(members):
            ref[m * edge:(m + 1) * edge, :] = con_ref[m, pl.ds(pl.multiple_of(at, 16), edge), :].astype(bf16)
        ref[members * edge:, :] = placed
    for m in range(members):
        low_ref[m * cells:(m + 1) * cells, :] = con_ref[m].astype(bf16)
    low_ref[members * cells:, :] = placed


def pick_kernel(lat_tile, blocks, info_ref, ens_ref, out_ref):
    members, cells, levels = ens_ref.shape
    slots = out_ref.shape[0]
    lon_pos = to_rows(lane_row(info_ref, 0, blocks, slots))
    lat_pos = to_rows(lane_row(info_ref, blocks, blocks, slots))
    cell_of = lon_pos * float(lat_tile) + lat_pos
    chosen = (fiota((slots, cells), 1) == cell_of).astype(bf16)
    for m in range(members):
        out_ref[:, m * levels:(m + 1) * levels] = dot(chosen, ens_ref[m]).astype(bf16)


def obs_by_cell(lon_pos, lat_pos, taps_lon, taps_lat, lon_count, lat_count, start):
    slots, rim = lon_pos.shape[0], taps_lon.shape[0] // 2
    wide = 128
    lon_w = band(fiota((slots, wide), 1) + (start + rim) - lon_pos, taps_lon)
    lat_w = band(fiota((slots, wide), 1) + rim - lat_pos, taps_lat)
    cells = lon_count * lat_count
    cell = fiota((wide, cells), 1)
    lon_of = jnp.floor((cell + 0.5) * (1.0 / lat_count))
    lat_of = cell - lon_of * float(lat_count)
    place = fiota((wide, cells), 0)
    lon_e = dot(lon_w.astype(bf16), (place == lon_of).astype(bf16))
    lat_e = dot(lat_w.astype(bf16), (place == lat_of).astype(bf16))
    return (lon_e * lat_e).astype(bf16)


def prep_kernel(dims, taps_lon, taps_lat, info_ref, *refs):
    lon_tile, lat_tile, rim, members, blocks = dims
    count = (len(refs) - 1) // 3
    tiles, base_ref, rims = refs[:count], refs[count], refs[count + 1:]
    slots, levels = base_ref.shape[0], tiles[0].shape[1]
    cells = lon_tile * lat_tile
    lon_pos = to_rows(lane_row(info_ref, 0, blocks, slots))
    lat_pos = to_rows(lane_row(info_ref, blocks, blocks, slots))
    for t, tile in enumerate(tiles):
        here = lat_pos if t == 0 else lat_pos - signs("lat")[t - 1] * float(lat_tile)
        weight = obs_by_cell(lon_pos, here, taps_lon, taps_lat, lon_tile, lat_tile, 0.0)
        for m in range(members):
            part = dot(weight, tile[m * cells:(m + 1) * cells, :])
            lanes = slice(m * levels, (m + 1) * levels)
            base_ref[:, lanes] = part if t == 0 else base_ref[:, lanes] + part
        for side, sign in enumerate(signs("lon")):
            off = jnp.where(sign > 0, float(lon_tile), float(-rim))
            rims[2 * t + side][...] = obs_by_cell(lon_pos, here, taps_lon, taps_lat, rim, lat_tile, off)


def part_kernel(blocks, base_ref, own_ref, values_ref, *refs):
    out_ref = refs[-1]
    count = len(refs) // 5
    tiles, weights, halos = refs[:count - 1], refs[count - 1:3 * count - 1], refs[3 * count - 1:-1]
    n_slots, levels = values_ref.shape
    slots, wide = base_ref.shape
    members = wide // levels
    block = weights[0].shape[1]
    total = jnp.zeros((slots, levels), f32)
    for m in range(members):
        lanes = slice(m * levels, (m + 1) * levels)
        spread = base_ref[:, lanes]
        for w, h in zip(weights, halos):
            spread += dot(w[...], h[m * block:(m + 1) * block, :])
        total += spread * own_ref[:, lanes].astype(f32)
    out_ref[slots:, :] = jnp.zeros((out_ref.shape[0] - slots, levels), f32)
    at = slots
    for t in range(count):
        for ref in (halos[2 * t], halos[2 * t + 1]) + ((tiles[t],) if t < count - 1 else ()):
            rows = ref[...] if ref.shape[0] == tail else ref[members * block:, :]
            out_ref[at:at + 2 * blocks, :] = rows.astype(f32)[0:2 * blocks]
            at += 2 * blocks
    out_ref[0:slots, :] = total
    mine = pl.ds(pl.multiple_of(lax.axis_index("mem") * n_slots, n_slots), n_slots)
    out_ref[mine, :] = out_ref[mine, :] - values_ref[...]


def resid_kernel(blocks, info_ref, own_ref, *refs):
    terms, (resid_ref, send_ref, extra_ref) = refs[:-3], refs[-3:]
    slots, wide = send_ref.shape
    levels = resid_ref.shape[1]
    weight = to_rows(lane_row(info_ref, 2 * blocks, blocks, slots))
    total = terms[0][...]
    for t in terms[1:]:
        total = total + t[...]
    resid = weight * total[0:slots]
    for m in range(wide // levels):
        lanes = slice(m * levels, (m + 1) * levels)
        send_ref[:, lanes] = (own_ref[:, lanes].astype(f32) * resid).astype(bf16)
    resid_ref[...] = resid
    extra_ref[...] = total[slots:]


def weight_kernel(dims, taps_lon, taps_lat, info_ref, extra_ref, resid_ref, out_ref, mine_ref):
    lon_tile, lat_tile, blocks, tiles = dims
    slots, levels = resid_ref.shape
    n_slots = mine_ref.shape[0]
    mine_ref[...] = resid_ref[pl.ds(pl.multiple_of(lax.axis_index("mem") * n_slots, n_slots), n_slots), :]
    rim = taps_lon.shape[0] // 2
    lon_sign, lat_sign = signs("lon"), signs("lat")
    at = 0
    lon_pos, lat_pos = [], []
    for t in range(tiles):
        shift = 0.0 if t == 0 else lat_sign[t - 1] * float(lat_tile)
        beside = []
        for side in range(2):
            beside.append((lane_row(extra_ref, at, blocks, slots) + lon_sign[side] * float(lon_tile), lane_row(extra_ref, at + blocks, blocks, slots)))
            at += 2 * blocks
        if t == 0:
            here = (lane_row(info_ref, 0, blocks, slots), lane_row(info_ref, blocks, blocks, slots))
        else:
            here = after
        if t + 1 < tiles:
            after = (lane_row(extra_ref, at, blocks, slots), lane_row(extra_ref, at + blocks, blocks, slots))
            at += 2 * blocks
        for lon_at, lat_at in [here] + beside:
            lon_pos.append(lon_at)
            lat_pos.append(lat_at + shift)
    lon_pos, lat_pos = jnp.concatenate(lon_pos, axis=1), jnp.concatenate(lat_pos, axis=1)
    tall = 32
    lon_w = band(fiota((tall, lon_pos.shape[1]), 0) + rim - lon_pos, taps_lon)
    lat_w = band(fiota((tall, lat_pos.shape[1]), 0) + rim - lat_pos, taps_lat)
    cells = lon_tile * lat_tile
    lon_of = fiota((lon_tile, lat_tile, tall), 0).reshape(cells, tall)
    lat_of = fiota((lon_tile, lat_tile, tall), 1).reshape(cells, tall)
    place = fiota((cells, tall), 1)
    lon_e = dot((place == lon_of).astype(bf16), lon_w.astype(bf16))
    lat_e = dot((place == lat_of).astype(bf16), lat_w.astype(bf16))
    out_ref[...] = (lon_e * lat_e).astype(bf16)


def back_kernel(weight_ref, con_ref, *refs):
    sets, out_ref, all_ref = refs[:-2], refs[-2], refs[-1]
    members, _, levels = con_ref.shape
    slots = sets[0].shape[0]
    for s, ref in enumerate(sets):
        all_ref[s * slots:(s + 1) * slots, :] = ref[...]
    back = dot(weight_ref[...], all_ref[...])
    for m in range(members):
        con = con_ref[m]
        out_ref[m] = con - descent * (con + back[:, m * levels:(m + 1) * levels])


def shards(controls, ensemble, taps_lon, taps_lat, obs_columns, obs_count, obs_quality, obs_values):
    rim = taps_lon.shape[0] // 2
    members, lon_tile, lat_tile, levels = controls.shape
    n_slots = obs_columns.shape[-1]
    n_mem = lax.axis_size("mem")
    slots = n_slots * n_mem
    blocks = (slots + levels - 1) // levels
    cells = lon_tile * lat_tile
    edge = rim * lat_tile
    wide = members * levels
    lon_pairs = pairings(lax.axis_size("lon"), True)
    lat_pairs = pairings(lax.axis_size("lat"), False)
    vmem = pl.BlockSpec(memory_space=pltpu.VMEM)
    smem = pl.BlockSpec(memory_space=pltpu.SMEM)
    shape = jax.ShapeDtypeStruct
    taps_lon = taps_lon.astype(bf16).astype(f32)
    taps_lat = taps_lat.astype(bf16).astype(f32)
    flat = controls.reshape(members, cells, levels)

    lanes = -(-(2 * n_slots + 1) // 128) * 128
    lane = lax.broadcasted_iota(jnp.int32, (1, 1, 1, lanes), 3)
    zeros = ((0, 0),) * 3
    raw = jnp.where(lane == 2 * n_slots, lax.broadcast_in_dim(obs_count, lane.shape, (0, 1, 2)), 0)
    raw += jnp.pad(obs_columns, zeros + ((0, lanes - n_slots),))
    raw += jnp.pad(obs_quality, zeros + ((n_slots, lanes - 2 * n_slots),))
    raw = raw.astype(f32).reshape(1, lanes)
    low, rim1, rim2, info = pl.pallas_call(
        functools.partial(start_kernel, (edge, lat_tile, n_slots, blocks)),
        out_shape=[shape((members * cells + tail, levels), bf16)] + [shape((members * edge + tail, levels), bf16)] * 2
        + [shape((up8(3 * blocks), levels), f32)],
        in_specs=[vmem] * 2, out_specs=[vmem] * 4, compiler_params=params(),
    )(flat, raw)
    halos = [lax.ppermute(r, "lon", p) for r, p in zip((rim1, rim2), lon_pairs)]
    tiles = [low] + [lax.ppermute(low, "lat", p) for p in lat_pairs]
    info = sum(sum_terms(info, n_mem, 2))
    n_rims = 2 * len(tiles)

    own = pl.pallas_call(
        functools.partial(pick_kernel, lat_tile, blocks),
        out_shape=shape((slots, wide), bf16),
        in_specs=[vmem] * 2, out_specs=vmem, compiler_params=params(),
    )(info, ensemble.reshape(members, cells, levels))
    base, *weights = pl.pallas_call(
        functools.partial(prep_kernel, (lon_tile, lat_tile, rim, members, blocks)),
        out_shape=[shape((slots, wide), f32)] + [shape((slots, edge), bf16)] * n_rims,
        in_specs=[smem] * 2 + [vmem] * (1 + len(tiles)), out_specs=[vmem] * (1 + n_rims), compiler_params=params(),
    )(taps_lon, taps_lat, info, *tiles)

    rims = list(halos)
    for p in lat_pairs:
        rims += [lax.ppermute(h, "lat", p) for h in halos]

    tall = slots + up8(2 * blocks * (3 * len(tiles) - 1))
    tails = [t[members * cells:] for t in tiles[1:]]
    mine = pl.pallas_call(
        functools.partial(part_kernel, blocks),
        out_shape=shape((tall, levels), f32),
        in_specs=[vmem] * (3 + len(tails) + 2 * len(rims)), out_specs=vmem, compiler_params=params(),
    )(base, own, obs_values.reshape(n_slots, levels), *tails, *weights, *rims)
    terms = sum_terms(mine, n_mem)

    resid, send, extra = pl.pallas_call(
        functools.partial(resid_kernel, blocks),
        out_shape=[shape((slots, levels), f32), shape((slots, wide), bf16), shape((tall - slots, levels), f32)],
        in_specs=[vmem] * (2 + len(terms)), out_specs=[vmem] * 3, compiler_params=params(),
    )(info, own, *terms)

    row = [send] + [lax.ppermute(send, "lon", p) for p in lon_pairs]
    count = len(row) * len(tiles)
    weight, resid = pl.pallas_call(
        functools.partial(weight_kernel, (lon_tile, lat_tile, blocks, len(tiles))),
        out_shape=[shape((cells, count * slots), bf16), shape((n_slots, levels), f32)],
        in_specs=[smem] * 2 + [vmem] * 3, out_specs=[vmem] * 2, compiler_params=params(),
    )(taps_lon, taps_lat, info, extra, resid)
    *late, weight = lax.optimization_barrier((*row[1:], weight))
    around = list(row)
    for q in lat_pairs:
        around += [lax.ppermute(r, "lat", q) for r in [send] + late]
    group = 2 if members % 2 == 0 else 1
    spec = pl.BlockSpec((group, cells, levels), lambda i: (i, 0, 0))
    part = pl.BlockSpec((slots, group * levels), lambda i: (0, i))
    whole = pl.BlockSpec((cells, count * slots), lambda i: (0, 0))
    new = pl.pallas_call(
        back_kernel,
        grid=(members // group,),
        out_shape=shape((members, cells, levels), f32),
        in_specs=[whole, spec] + [part] * count, out_specs=spec,
        scratch_shapes=[pltpu.VMEM((count * slots, group * levels), bf16)],
        compiler_params=params(),
    )(weight, flat, *around)
    return (new.reshape(controls.shape), resid[None, None, None])


def solution(mesh):
    placed = (
        P("mem", "lon", "lat", None),
        P("mem", "lon", "lat", None),
        P(),
        P(),
        P("lon", "lat", "mem", None),
        P("lon", "lat", "mem"),
        P("lon", "lat", "mem", None),
        P("lon", "lat", "mem", None, None),
    )
    return jax.shard_map(
        shards,
        mesh=mesh,
        in_specs=placed,
        out_specs=(P("mem", "lon", "lat", None), P("lon", "lat", "mem", None, None)),
        check_vma=False,
    )
```

```python
import functools

import jax
import jax.numpy as jnp
from jax import lax
from jax.experimental import pallas as pl
from jax.experimental.pallas import tpu as pltpu
from jax.sharding import PartitionSpec as P

descent = 0.5
f32 = jnp.float32
bf16 = jnp.bfloat16
tail = 16


def pairings(size, wraps):
    even = [(i, i ^ 1) for i in range(size)]
    odd = []
    for i in range(size):
        j = i + 1 if i % 2 else i - 1
        if wraps:
            j = j % size
        if 0 <= j < size:
            odd.append((i, j))
    return [even, odd] if odd else [even]


def sum_terms(x, count):
    if count <= 4:
        return [x] + [lax.ppermute(x, "mem", [(i, i ^ b) for i in range(count)]) for b in range(1, count)]
    step = 1
    while step < count:
        other = lax.ppermute(x, "mem", [(i, i ^ step) for i in range(count)])
        step *= 2
        if step < count:
            x = x + other
    return [x, other]


def up8(n):
    return (n + 7) // 8 * 8


def signs(axis):
    even = lax.axis_index(axis) % 2 == 0
    return [jnp.where(even, 1.0, -1.0).astype(f32), jnp.where(even, -1.0, 1.0).astype(f32)]


def fiota(shape, dim):
    return lax.broadcasted_iota(jnp.int32, shape, dim).astype(f32)


def diagonal(rows, lanes, shift=0.0):
    return fiota((rows, lanes), 0) + shift == fiota((rows, lanes), 1)


def to_rows(lanes):
    n = lanes.shape[1]
    return jnp.sum(jnp.where(diagonal(n, n), lanes, 0.0), axis=1, keepdims=True)


def to_lanes(rows):
    n = rows.shape[0]
    return jnp.sum(jnp.where(diagonal(n, n), rows, 0.0), axis=0, keepdims=True)


def owner_lanes(lanes, first, width):
    here = diagonal(lanes.shape[1], width, first.astype(f32))
    return jnp.sum(jnp.where(here, to_rows(lanes), 0.0), axis=0, keepdims=True)


def lane_row(ref, first, blocks, slots):
    if blocks == 1:
        return ref[first:first + 1, 0:slots]
    return jnp.concatenate([ref[first + r:first + r + 1, :] for r in range(blocks)], axis=1)[:, 0:slots]


def band(distance, taps_ref):
    out = jnp.zeros_like(distance)
    for k in range(taps_ref.shape[0]):
        out = jnp.where(distance == float(k), taps_ref[k], out)
    return out


def dot(a, b):
    return jnp.dot(a, b, preferred_element_type=f32)


def params(mib=32):
    return pltpu.CompilerParams(vmem_limit_bytes=mib * 1024 * 1024)


def start_kernel(dims, con_ref, col_ref, low_ref, rim1_ref, rim2_ref, info_ref, *side_refs):
    rim, lon_tile, lat_tile, blocks = dims
    edge = rim * lat_tile
    members, cells, levels = con_ref.shape
    n_slots = col_ref.shape[1]
    mem = lax.axis_index("mem")
    column = col_ref[...].astype(f32)
    lon_pos = jnp.floor((column + 0.5) * (1.0 / lat_tile))
    lat_pos = column - lon_pos * float(lat_tile)
    info_ref[...] = jnp.zeros_like(info_ref)
    row = lax.broadcasted_iota(jnp.int32, (tail, levels), 0)
    placed = jnp.zeros((tail, levels), f32)
    for f, lanes in enumerate((lon_pos, lat_pos)):
        for r in range(blocks):
            moved = owner_lanes(lanes, mem * n_slots - r * levels, levels)
            info_ref[f * blocks + r:f * blocks + r + 1, :] = moved
            placed = jnp.where(row == f * blocks + r, moved, placed)
    placed = placed.astype(bf16)
    even = lax.axis_index("lon") % 2 == 0
    far = cells - edge
    for at, ref in ((jnp.where(even, far, 0), rim1_ref), (jnp.where(even, 0, far), rim2_ref)):
        for m in range(members):
            ref[m * edge:(m + 1) * edge, :] = con_ref[m, pl.ds(pl.multiple_of(at, 16), edge), :].astype(bf16)
        ref[members * edge:, :] = placed
    for ref, sign in zip(side_refs, signs("lat")):
        at = jnp.where(sign > 0, lat_tile - rim, 0)
        for m in range(members):
            for i in range(0, lon_tile, 2):
                pair = [con_ref[m, pl.ds(pl.multiple_of(at + (i + k) * lat_tile, 8), rim), :] for k in range(2)]
                row_at = (m * lon_tile + i) * rim
                ref[row_at:row_at + 2 * rim, :] = jnp.concatenate(pair, axis=0).astype(bf16)
        ref[members * lon_tile * rim:, :] = placed
    for m in range(members):
        low_ref[m * cells:(m + 1) * cells, :] = con_ref[m].astype(bf16)


def pick_kernel(lat_tile, blocks, info_ref, ens_ref, out_ref):
    members, cells, levels = ens_ref.shape
    slots = out_ref.shape[0]
    lon_pos = to_rows(lane_row(info_ref, 0, blocks, slots))
    lat_pos = to_rows(lane_row(info_ref, blocks, blocks, slots))
    cell_of = lon_pos * float(lat_tile) + lat_pos
    chosen = (fiota((slots, cells), 1) == cell_of).astype(bf16)
    for m in range(members):
        out_ref[:, m * levels:(m + 1) * levels] = dot(chosen, ens_ref[m]).astype(bf16)


def prep_kernel(dims, taps_lon, taps_lat, info_ref, low_ref, *refs):
    lon_tile, lat_tile, rim, members, blocks = dims
    count = (len(refs) - 3) // 3
    sides, base_ref, rims = refs[:count], refs[count], refs[count + 1:]
    slots, levels = base_ref.shape[0], low_ref.shape[1]
    cells, edge, flank = lon_tile * lat_tile, rim * lat_tile, rim * lon_tile
    lon_pos = to_rows(lane_row(info_ref, 0, blocks, slots))
    lat_pos = to_rows(lane_row(info_ref, blocks, blocks, slots))
    lane = fiota((slots, 128), 1)
    lon_w = band(lane - lon_pos, taps_lon).astype(bf16)
    lat_w = band(lane + float(rim - lat_tile) - lat_pos, taps_lat).astype(bf16)
    lon_side = [jnp.where(s > 0, float(lon_tile), float(-rim)) for s in signs("lon")]
    sections = [(cells, 0.0, 0.0, lat_tile)] + [(edge, o, 0.0, lat_tile) for o in lon_side]
    for s in signs("lat")[:count]:
        sections += [(edge, o, s * float(lat_tile), lat_tile) for o in lon_side]
        sections.append((flank, 0.0, jnp.where(s > 0, float(lat_tile), float(-rim)), rim))
    lon_at, lat_at = [], []
    for size, lon_off, lat_off, width in sections:
        cell = fiota((1, -(-size // 128) * 128), 1)
        lon_of = jnp.floor((cell + 0.5) * (1.0 / width))
        lon_at.append(jnp.where(cell < size, lon_of + (lon_off + float(rim)), -1.0))
        lat_at.append(cell - lon_of * float(width) + (lat_off + float(lat_tile)))
    lon_at, lat_at = jnp.concatenate(lon_at, axis=1), jnp.concatenate(lat_at, axis=1)
    place = fiota((128, lon_at.shape[1]), 0)
    lon_e = dot(lon_w[:, 0:64], (place[0:64] == lon_at).astype(bf16))
    lat_e = dot(lat_w, (place == lat_at).astype(bf16))
    weight = (lon_e * lat_e).astype(bf16)
    ends = [0]
    for size, _, _, _ in sections:
        ends.append(ends[-1] + -(-size // 128) * 128)
    pieces = [weight[:, e:e + section[0]] for e, section in zip(ends, sections)]
    for m in range(members):
        part = dot(pieces[0], low_ref[m * cells:(m + 1) * cells, :])
        for t, side in enumerate(sides):
            part += dot(pieces[3 * t + 5], side[m * flank:(m + 1) * flank, :])
        base_ref[:, m * levels:(m + 1) * levels] = part
    kept = pieces[1:3]
    for t in range(count):
        kept += pieces[3 * t + 3:3 * t + 5]
    for ref, piece in zip(rims, kept):
        ref[...] = piece


def part_kernel(blocks, base_ref, own_ref, values_ref, scale_ref, *refs):
    out_ref = refs[-1]
    count = len(refs) // 5
    tiles, weights, halos = refs[:count - 1], refs[count - 1:3 * count - 1], refs[3 * count - 1:-1]
    n_slots, levels = values_ref.shape
    slots, wide = base_ref.shape
    members = wide // levels
    block = weights[0].shape[1]
    total = jnp.zeros((slots, levels), f32)
    for m in range(members):
        lanes = slice(m * levels, (m + 1) * levels)
        spread = base_ref[:, lanes]
        for w, h in zip(weights, halos):
            spread += dot(w[...], h[m * block:(m + 1) * block, :])
        total += spread * own_ref[:, lanes].astype(f32)
    out_ref[slots:, :] = jnp.zeros((out_ref.shape[0] - slots, levels), f32)
    at = slots
    for t in range(count):
        for ref in (halos[2 * t], halos[2 * t + 1]) + ((tiles[t],) if t < count - 1 else ()):
            rows = ref[...] if ref.shape[0] == tail else ref[members * block:, :]
            out_ref[at:at + 2 * blocks, :] = rows.astype(f32)[0:2 * blocks]
            at += 2 * blocks
    mem = lax.axis_index("mem")
    for r in range(blocks):
        out_ref[at + r:at + r + 1, :] = owner_lanes(scale_ref[...], mem * n_slots - r * levels, levels)
    out_ref[0:slots, :] = total
    mine = pl.ds(pl.multiple_of(mem * n_slots, n_slots), n_slots)
    out_ref[mine, :] = out_ref[mine, :] - values_ref[...]


def resid_kernel(blocks, tiles, own_ref, *refs):
    terms, (resid_ref, send_ref, extra_ref) = refs[:-3], refs[-3:]
    slots, wide = send_ref.shape
    levels = resid_ref.shape[1]
    total = terms[0][...]
    for t in terms[1:]:
        total = total + t[...]
    extra_ref[...] = total[slots:]
    resid = to_rows(lane_row(extra_ref, 2 * blocks * (3 * tiles - 1), blocks, slots)) * total[0:slots]
    for m in range(wide // levels):
        lanes = slice(m * levels, (m + 1) * levels)
        send_ref[:, lanes] = (own_ref[:, lanes].astype(f32) * resid).astype(bf16)
    resid_ref[...] = resid


def weight_kernel(dims, taps_lon, taps_lat, info_ref, extra_ref, resid_ref, out_ref, mine_ref):
    lon_tile, lat_tile, blocks, tiles = dims
    slots, levels = resid_ref.shape
    n_slots = mine_ref.shape[0]
    mine_ref[...] = resid_ref[pl.ds(pl.multiple_of(lax.axis_index("mem") * n_slots, n_slots), n_slots), :]
    rim = taps_lon.shape[0] // 2
    lon_sign, lat_sign = signs("lon"), signs("lat")
    at = 0
    lon_pos, lat_pos = [], []
    for t in range(tiles):
        shift = 0.0 if t == 0 else lat_sign[t - 1] * float(lat_tile)
        beside = []
        for side in range(2):
            beside.append((lane_row(extra_ref, at, blocks, slots) + lon_sign[side] * float(lon_tile), lane_row(extra_ref, at + blocks, blocks, slots)))
            at += 2 * blocks
        if t == 0:
            here = (lane_row(info_ref, 0, blocks, slots), lane_row(info_ref, blocks, blocks, slots))
        else:
            here = after
        if t + 1 < tiles:
            after = (lane_row(extra_ref, at, blocks, slots), lane_row(extra_ref, at + blocks, blocks, slots))
            at += 2 * blocks
        for lon_at, lat_at in [here] + beside:
            lon_pos.append(lon_at)
            lat_pos.append(lat_at + shift)
    lon_pos, lat_pos = jnp.concatenate(lon_pos, axis=1), jnp.concatenate(lat_pos, axis=1)
    tall = 32
    lon_w = band(fiota((tall, lon_pos.shape[1]), 0) + rim - lon_pos, taps_lon)
    lat_w = band(fiota((tall, lat_pos.shape[1]), 0) + rim - lat_pos, taps_lat)
    cells = lon_tile * lat_tile
    lon_of = fiota((lon_tile, lat_tile, tall), 0).reshape(cells, tall)
    lat_of = fiota((lon_tile, lat_tile, tall), 1).reshape(cells, tall)
    place = fiota((cells, tall), 1)
    lon_e = dot((place == lon_of).astype(bf16), lon_w.astype(bf16))
    lat_e = dot((place == lat_of).astype(bf16), lat_w.astype(bf16))
    out_ref[...] = (lon_e * lat_e).astype(bf16)


def back_kernel(group, pieces, weight_ref, con_ref, *refs):
    sets, out_hbm, all_ref, buf, sem = refs[:-4], refs[-4], refs[-3], refs[-2], refs[-1]
    members, cells, levels = con_ref.shape
    slots = sets[0].shape[0]
    for s, ref in enumerate(sets):
        all_ref[s * slots:(s + 1) * slots, :] = ref[...]
    step = cells // pieces
    copies = []
    for g in range(members // group):
        back = dot(weight_ref[...], all_ref[:, g * group * levels:(g + 1) * group * levels])
        for k in range(group):
            m = g * group + k
            for p in range(pieces):
                rows = slice(p * step, (p + 1) * step)
                con = con_ref[m, rows, :]
                buf[m, rows, :] = con - descent * (con + back[rows, k * levels:(k + 1) * levels])
                copies.append(pltpu.make_async_copy(buf.at[m, rows], out_hbm.at[m, rows], sem.at[m * pieces + p]))
                copies[-1].start()
    for copy in copies:
        copy.wait()


def shards(controls, ensemble, taps_lon, taps_lat, obs_columns, obs_count, obs_quality, obs_values):
    rim = taps_lon.shape[0] // 2
    members, lon_tile, lat_tile, levels = controls.shape
    n_slots = obs_columns.shape[-1]
    n_mem = lax.axis_size("mem")
    slots = n_slots * n_mem
    blocks = (slots + levels - 1) // levels
    cells = lon_tile * lat_tile
    edge = rim * lat_tile
    wide = members * levels
    lon_pairs = pairings(lax.axis_size("lon"), True)
    lat_pairs = pairings(lax.axis_size("lat"), False)
    vmem = pl.BlockSpec(memory_space=pltpu.VMEM)
    smem = pl.BlockSpec(memory_space=pltpu.SMEM)
    shape = jax.ShapeDtypeStruct
    taps_lon = taps_lon.astype(bf16).astype(f32)
    taps_lat = taps_lat.astype(bf16).astype(f32)
    flat = controls.reshape(members, cells, levels)

    flank = rim * lon_tile
    low, rim1, rim2, info, *sides = pl.pallas_call(
        functools.partial(start_kernel, (rim, lon_tile, lat_tile, blocks)),
        out_shape=[shape((members * cells, levels), bf16)] + [shape((members * edge + tail, levels), bf16)] * 2
        + [shape((up8(2 * blocks), levels), f32)] + [shape((members * flank + tail, levels), bf16)] * len(lat_pairs),
        in_specs=[vmem] * 2, out_specs=[vmem] * (4 + len(lat_pairs)), compiler_params=params(),
    )(flat, obs_columns.reshape(1, n_slots))
    halos = [lax.ppermute(r, "lon", p) for r, p in zip((rim1, rim2), lon_pairs)]
    sides = [lax.ppermute(r, "lat", p) for r, p in zip(sides, lat_pairs)]
    n_tiles = 1 + len(lat_pairs)
    live = lax.broadcasted_iota(jnp.int32, (1, n_slots), 1) < obs_count[0]
    scale = jnp.where(live, 0.5 * obs_quality[0, 0].astype(f32), 0.0)
    info, scale = lax.optimization_barrier((info, scale))
    step = 1
    while step < n_mem:
        info = info + lax.ppermute(info, "mem", [(i, i ^ step) for i in range(n_mem)])
        step *= 2
    n_rims = 2 * n_tiles

    own = pl.pallas_call(
        functools.partial(pick_kernel, lat_tile, blocks),
        out_shape=shape((slots, wide), bf16),
        in_specs=[vmem] * 2, out_specs=vmem, compiler_params=params(),
    )(info, ensemble.reshape(members, cells, levels))
    base, *weights = pl.pallas_call(
        functools.partial(prep_kernel, (lon_tile, lat_tile, rim, members, blocks)),
        out_shape=[shape((slots, wide), f32)] + [shape((slots, edge), bf16)] * n_rims,
        in_specs=[smem] * 2 + [vmem] * (1 + n_tiles), out_specs=[vmem] * (1 + n_rims), compiler_params=params(),
    )(taps_lon, taps_lat, info, low, *sides)

    rims = list(halos)
    for p in lat_pairs:
        rims += [lax.ppermute(h, "lat", p) for h in halos]

    tall = slots + up8(2 * blocks * (3 * n_tiles - 1) + blocks)
    tails = [t[members * flank:] for t in sides]
    mine = pl.pallas_call(
        functools.partial(part_kernel, blocks),
        out_shape=shape((tall, levels), f32),
        in_specs=[vmem] * (4 + len(tails) + 2 * len(rims)), out_specs=vmem, compiler_params=params(),
    )(base, own, obs_values.reshape(n_slots, levels), scale, *tails, *weights, *rims)
    terms = sum_terms(mine, n_mem)

    resid, send, extra = pl.pallas_call(
        functools.partial(resid_kernel, blocks, n_tiles),
        out_shape=[shape((slots, levels), f32), shape((slots, wide), bf16), shape((tall - slots, levels), f32)],
        in_specs=[vmem] * (1 + len(terms)), out_specs=[vmem] * 3, compiler_params=params(),
    )(own, *terms)

    row = [send] + [lax.ppermute(send, "lon", p) for p in lon_pairs]
    count = len(row) * n_tiles
    weight, resid = pl.pallas_call(
        functools.partial(weight_kernel, (lon_tile, lat_tile, blocks, n_tiles)),
        out_shape=[shape((cells, count * slots), bf16), shape((n_slots, levels), f32)],
        in_specs=[smem] * 2 + [vmem] * 3, out_specs=[vmem] * 2, compiler_params=params(),
    )(taps_lon, taps_lat, info, extra, resid)
    row[1], weight = lax.optimization_barrier((row[1], weight))
    around = list(row)
    for q in lat_pairs:
        around += [lax.ppermute(r, "lat", q) for r in row]
    group = 2 if members % 2 == 0 else 1
    pieces = 2
    new = pl.pallas_call(
        functools.partial(back_kernel, group, pieces),
        out_shape=shape((members, cells, levels), f32),
        in_specs=[vmem] * (2 + count), out_specs=pl.BlockSpec(memory_space=pl.ANY),
        scratch_shapes=[
            pltpu.VMEM((count * slots, wide), bf16),
            pltpu.VMEM((members, cells, levels), f32),
            pltpu.SemaphoreType.DMA((members * pieces,)),
        ],
        compiler_params=params(),
    )(weight, flat, *around)
    return (new.reshape(controls.shape), resid[None, None, None])


def solution(mesh):
    placed = (
        P("mem", "lon", "lat", None),
        P("mem", "lon", "lat", None),
        P(),
        P(),
        P("lon", "lat", "mem", None),
        P("lon", "lat", "mem"),
        P("lon", "lat", "mem", None),
        P("lon", "lat", "mem", None, None),
    )
    return jax.shard_map(
        shards,
        mesh=mesh,
        in_specs=placed,
        out_specs=(P("mem", "lon", "lat", None), P("lon", "lat", "mem", None, None)),
        check_vma=False,
    )
```

```python
import functools

import jax
import jax.numpy as jnp
from jax import lax
from jax.experimental import pallas as pl
from jax.experimental.pallas import tpu as pltpu
from jax.sharding import PartitionSpec as P

descent = 0.5
f32 = jnp.float32
bf16 = jnp.bfloat16
tail = 16


def pairings(size, wraps):
    even = [(i, i ^ 1) for i in range(size)]
    odd = []
    for i in range(size):
        j = i + 1 if i % 2 else i - 1
        if wraps:
            j = j % size
        if 0 <= j < size:
            odd.append((i, j))
    return [even, odd] if odd else [even]


def sum_terms(x, count):
    if count <= 4:
        return [x] + [lax.ppermute(x, "mem", [(i, i ^ b) for i in range(count)]) for b in range(1, count)]
    step = 1
    while step < count:
        other = lax.ppermute(x, "mem", [(i, i ^ step) for i in range(count)])
        step *= 2
        if step < count:
            x = x + other
    return [x, other]


def up8(n):
    return (n + 7) // 8 * 8


def signs(axis):
    even = lax.axis_index(axis) % 2 == 0
    return [jnp.where(even, 1.0, -1.0).astype(f32), jnp.where(even, -1.0, 1.0).astype(f32)]


def fiota(shape, dim):
    return lax.broadcasted_iota(jnp.int32, shape, dim).astype(f32)


def diagonal(rows, lanes, shift=0.0):
    return fiota((rows, lanes), 0) + shift == fiota((rows, lanes), 1)


def to_rows(lanes):
    n = lanes.shape[1]
    return jnp.sum(jnp.where(diagonal(n, n), lanes, 0.0), axis=1, keepdims=True)


def to_lanes(rows):
    n = rows.shape[0]
    return jnp.sum(jnp.where(diagonal(n, n), rows, 0.0), axis=0, keepdims=True)


def owner_lanes(lanes, first, width):
    here = diagonal(lanes.shape[1], width, first.astype(f32))
    return jnp.sum(jnp.where(here, to_rows(lanes), 0.0), axis=0, keepdims=True)


def lane_row(ref, first, blocks, slots):
    if blocks == 1:
        return ref[first:first + 1, 0:slots]
    return jnp.concatenate([ref[first + r:first + r + 1, :] for r in range(blocks)], axis=1)[:, 0:slots]


def band(distance, taps_ref):
    out = jnp.zeros_like(distance)
    for k in range(taps_ref.shape[0]):
        out = jnp.where(distance == float(k), taps_ref[k], out)
    return out


def dot(a, b):
    return jnp.dot(a, b, preferred_element_type=f32)


def params(mib=32):
    return pltpu.CompilerParams(vmem_limit_bytes=mib * 1024 * 1024)


def start_kernel(dims, con_ref, col_ref, low_ref, rim1_ref, rim2_ref, info_ref, *side_refs):
    rim, lon_tile, lat_tile, blocks = dims
    edge = rim * lat_tile
    members, cells, levels = con_ref.shape
    n_slots = col_ref.shape[1]
    mem = lax.axis_index("mem")
    column = col_ref[...].astype(f32)
    lon_pos = jnp.floor((column + 0.5) * (1.0 / lat_tile))
    lat_pos = column - lon_pos * float(lat_tile)
    info_ref[...] = jnp.zeros_like(info_ref)
    row = lax.broadcasted_iota(jnp.int32, (tail, levels), 0)
    placed = jnp.zeros((tail, levels), f32)
    for f, lanes in enumerate((lon_pos, lat_pos)):
        for r in range(blocks):
            moved = owner_lanes(lanes, mem * n_slots - r * levels, levels)
            info_ref[f * blocks + r:f * blocks + r + 1, :] = moved
            placed = jnp.where(row == f * blocks + r, moved, placed)
    placed = placed.astype(bf16)
    even = lax.axis_index("lon") % 2 == 0
    far = cells - edge
    for at, ref in ((jnp.where(even, far, 0), rim1_ref), (jnp.where(even, 0, far), rim2_ref)):
        for m in range(members):
            ref[m * edge:(m + 1) * edge, :] = con_ref[m, pl.ds(pl.multiple_of(at, 16), edge), :].astype(bf16)
        ref[members * edge:, :] = placed
    for ref, sign in zip(side_refs, signs("lat")):
        at = jnp.where(sign > 0, lat_tile - rim, 0)
        for m in range(members):
            for i in range(0, lon_tile, 2):
                pair = [con_ref[m, pl.ds(pl.multiple_of(at + (i + k) * lat_tile, 8), rim), :] for k in range(2)]
                row_at = (m * lon_tile + i) * rim
                ref[row_at:row_at + 2 * rim, :] = jnp.concatenate(pair, axis=0).astype(bf16)
        ref[members * lon_tile * rim:, :] = placed
    for m in range(members):
        low_ref[m * cells:(m + 1) * cells, :] = con_ref[m].astype(bf16)


def pick_kernel(lat_tile, blocks, info_ref, ens_ref, out_ref):
    members, cells, levels = ens_ref.shape
    slots = out_ref.shape[0]
    lon_pos = to_rows(lane_row(info_ref, 0, blocks, slots))
    lat_pos = to_rows(lane_row(info_ref, blocks, blocks, slots))
    cell_of = lon_pos * float(lat_tile) + lat_pos
    chosen = (fiota((slots, cells), 1) == cell_of).astype(bf16)
    for m in range(members):
        out_ref[:, m * levels:(m + 1) * levels] = dot(chosen, ens_ref[m]).astype(bf16)


def prep_kernel(dims, taps_lon, taps_lat, info_ref, low_ref, *refs):
    lon_tile, lat_tile, rim, members, blocks = dims
    count = (len(refs) - 3) // 3
    sides, base_ref, rims = refs[:count], refs[count], refs[count + 1:]
    slots, levels = base_ref.shape[0], low_ref.shape[1]
    cells, edge, flank = lon_tile * lat_tile, rim * lat_tile, rim * lon_tile
    lon_pos = to_rows(lane_row(info_ref, 0, blocks, slots))
    lat_pos = to_rows(lane_row(info_ref, blocks, blocks, slots))
    lane = fiota((slots, 128), 1)
    lon_w = band(lane - lon_pos, taps_lon).astype(bf16)
    lat_w = band(lane + float(rim - lat_tile) - lat_pos, taps_lat).astype(bf16)
    lon_side = [jnp.where(s > 0, float(lon_tile), float(-rim)) for s in signs("lon")]
    sections = [(cells, 0.0, 0.0, lat_tile)] + [(edge, o, 0.0, lat_tile) for o in lon_side]
    for s in signs("lat")[:count]:
        sections += [(edge, o, s * float(lat_tile), lat_tile) for o in lon_side]
        sections.append((flank, 0.0, jnp.where(s > 0, float(lat_tile), float(-rim)), rim))
    lon_at, lat_at = [], []
    for size, lon_off, lat_off, width in sections:
        cell = fiota((1, -(-size // 128) * 128), 1)
        lon_of = jnp.floor((cell + 0.5) * (1.0 / width))
        lon_at.append(jnp.where(cell < size, lon_of + (lon_off + float(rim)), -1.0))
        lat_at.append(cell - lon_of * float(width) + (lat_off + float(lat_tile)))
    lon_at, lat_at = jnp.concatenate(lon_at, axis=1), jnp.concatenate(lat_at, axis=1)
    place = fiota((128, lon_at.shape[1]), 0)
    lon_e = dot(lon_w[:, 0:64], (place[0:64] == lon_at).astype(bf16))
    lat_e = dot(lat_w, (place == lat_at).astype(bf16))
    weight = (lon_e * lat_e).astype(bf16)
    ends = [0]
    for size, _, _, _ in sections:
        ends.append(ends[-1] + -(-size // 128) * 128)
    pieces = [weight[:, e:e + section[0]] for e, section in zip(ends, sections)]
    for m in range(members):
        part = dot(pieces[0], low_ref[m * cells:(m + 1) * cells, :])
        for t, side in enumerate(sides):
            part += dot(pieces[3 * t + 5], side[m * flank:(m + 1) * flank, :])
        base_ref[:, m * levels:(m + 1) * levels] = part
    kept = pieces[1:3]
    for t in range(count):
        kept += pieces[3 * t + 3:3 * t + 5]
    for ref, piece in zip(rims, kept):
        ref[...] = piece


def part_kernel(blocks, base_ref, own_ref, values_ref, scale_ref, *refs):
    out_ref = refs[-1]
    count = len(refs) // 5
    tiles, weights, halos = refs[:count - 1], refs[count - 1:3 * count - 1], refs[3 * count - 1:-1]
    n_slots, levels = values_ref.shape
    slots, wide = base_ref.shape
    members = wide // levels
    block = weights[0].shape[1]
    total = jnp.zeros((slots, levels), f32)
    for m in range(members):
        lanes = slice(m * levels, (m + 1) * levels)
        spread = base_ref[:, lanes]
        for w, h in zip(weights, halos):
            spread += dot(w[...], h[m * block:(m + 1) * block, :])
        total += spread * own_ref[:, lanes].astype(f32)
    out_ref[slots:, :] = jnp.zeros((out_ref.shape[0] - slots, levels), f32)
    at = slots
    for t in range(count):
        for ref in (halos[2 * t], halos[2 * t + 1]) + ((tiles[t],) if t < count - 1 else ()):
            rows = ref[...] if ref.shape[0] == tail else ref[members * block:, :]
            out_ref[at:at + 2 * blocks, :] = rows.astype(f32)[0:2 * blocks]
            at += 2 * blocks
    mem = lax.axis_index("mem")
    for r in range(blocks):
        out_ref[at + r:at + r + 1, :] = owner_lanes(scale_ref[...], mem * n_slots - r * levels, levels)
    out_ref[0:slots, :] = total
    mine = pl.ds(pl.multiple_of(mem * n_slots, n_slots), n_slots)
    out_ref[mine, :] = out_ref[mine, :] - values_ref[...]


def resid_kernel(blocks, tiles, own_ref, *refs):
    terms, (resid_ref, send_ref, extra_ref) = refs[:-3], refs[-3:]
    slots, wide = send_ref.shape
    levels = resid_ref.shape[1]
    total = terms[0][...]
    for t in terms[1:]:
        total = total + t[...]
    extra_ref[...] = total[slots:]
    resid = to_rows(lane_row(extra_ref, 2 * blocks * (3 * tiles - 1), blocks, slots)) * total[0:slots]
    for m in range(wide // levels):
        lanes = slice(m * levels, (m + 1) * levels)
        send_ref[:, lanes] = (own_ref[:, lanes].astype(f32) * resid).astype(bf16)
    resid_ref[...] = resid


def weight_kernel(dims, taps_lon, taps_lat, info_ref, extra_ref, resid_ref, out_ref, mine_ref):
    lon_tile, lat_tile, blocks, tiles = dims
    slots, levels = resid_ref.shape
    n_slots = mine_ref.shape[0]
    mine_ref[...] = resid_ref[pl.ds(pl.multiple_of(lax.axis_index("mem") * n_slots, n_slots), n_slots), :]
    rim = taps_lon.shape[0] // 2
    lon_sign, lat_sign = signs("lon"), signs("lat")
    at = 0
    placed = []
    for t in range(tiles):
        shift = 0.0 if t == 0 else lat_sign[t - 1] * float(lat_tile)
        beside = []
        for side in range(2):
            beside.append((lane_row(extra_ref, at, blocks, slots) + lon_sign[side] * float(lon_tile), lane_row(extra_ref, at + blocks, blocks, slots)))
            at += 2 * blocks
        if t == 0:
            here = (lane_row(info_ref, 0, blocks, slots), lane_row(info_ref, blocks, blocks, slots))
        else:
            here = after
        if t + 1 < tiles:
            after = (lane_row(extra_ref, at, blocks, slots), lane_row(extra_ref, at + blocks, blocks, slots))
            at += 2 * blocks
        placed.append([(lon_at, lat_at + shift) for lon_at, lat_at in [here] + beside])
    lon_pos = [placed[t][k][0] for k in range(3) for t in range(tiles)]
    lat_pos = [placed[t][k][1] for k in range(3) for t in range(tiles)]
    lon_pos, lat_pos = jnp.concatenate(lon_pos, axis=1), jnp.concatenate(lat_pos, axis=1)
    tall = 32
    lon_w = band(fiota((tall, lon_pos.shape[1]), 0) + rim - lon_pos, taps_lon)
    lat_w = band(fiota((tall, lat_pos.shape[1]), 0) + rim - lat_pos, taps_lat)
    cells = lon_tile * lat_tile
    lon_of = fiota((lon_tile, lat_tile, tall), 0).reshape(cells, tall)
    lat_of = fiota((lon_tile, lat_tile, tall), 1).reshape(cells, tall)
    place = fiota((cells, tall), 1)
    lon_e = dot((place == lon_of).astype(bf16), lon_w.astype(bf16))
    lat_e = dot((place == lat_of).astype(bf16), lat_w.astype(bf16))
    out_ref[...] = (lon_e * lat_e).astype(bf16)


def begin_kernel(group, edge, weight_ref, con_ref, *refs):
    sets, out_hbm, rest_ref, all_ref, buf, sem = refs[:-5], refs[-5], refs[-4], refs[-3], refs[-2], refs[-1]
    members, cells, levels = con_ref.shape
    slots = sets[0].shape[0]
    for s, ref in enumerate(sets):
        all_ref[s * slots:(s + 1) * slots, :] = ref[...]
    depth = len(sets) * slots
    last = signs("lon")[1] > 0
    done = pl.ds(pl.multiple_of(jnp.where(last, 0, edge), 16), cells - edge)
    left = pl.ds(pl.multiple_of(jnp.where(last, cells - edge, 0), 16), edge)
    copies = []
    for m in range(0, members, group):
        back = dot(weight_ref[:, 0:depth], all_ref[:, m * levels:(m + group) * levels])
        for k in range(group):
            con = con_ref[m + k]
            buf[m + k] = con - descent * (con + back[:, k * levels:(k + 1) * levels])
            copies.append(pltpu.make_async_copy(buf.at[m + k, done], out_hbm.at[m + k, done], sem.at[m + k]))
            copies[-1].start()
    for m in range(members):
        rest_ref[m] = buf[m, left, :]
    for copy in copies:
        copy.wait()


def end_kernel(group, weight_ref, rest_ref, begun_hbm, *refs):
    sets, out_hbm, all_ref, buf, sem = refs[:-4], refs[-4], refs[-3], refs[-2], refs[-1]
    members, edge, levels = rest_ref.shape
    cells = weight_ref.shape[0]
    slots = sets[0].shape[0]
    for s, ref in enumerate(sets):
        all_ref[s * slots:(s + 1) * slots, :] = ref[...]
    begin = weight_ref.shape[1] - len(sets) * slots
    left = pl.ds(pl.multiple_of(jnp.where(signs("lon")[1] > 0, cells - edge, 0), 16), edge)
    weight = weight_ref[left, begin:]
    copies = []
    for m in range(0, members, group):
        back = dot(weight, all_ref[:, m * levels:(m + group) * levels])
        for k in range(group):
            buf[m + k] = rest_ref[m + k] - descent * back[:, k * levels:(k + 1) * levels]
            copies.append(pltpu.make_async_copy(buf.at[m + k], out_hbm.at[m + k, left], sem.at[m + k]))
            copies[-1].start()
    for copy in copies:
        copy.wait()


def shards(controls, ensemble, taps_lon, taps_lat, obs_columns, obs_count, obs_quality, obs_values):
    rim = taps_lon.shape[0] // 2
    members, lon_tile, lat_tile, levels = controls.shape
    n_slots = obs_columns.shape[-1]
    n_mem = lax.axis_size("mem")
    slots = n_slots * n_mem
    blocks = (slots + levels - 1) // levels
    cells = lon_tile * lat_tile
    edge = rim * lat_tile
    wide = members * levels
    lon_pairs = pairings(lax.axis_size("lon"), True)
    lat_pairs = pairings(lax.axis_size("lat"), False)
    vmem = pl.BlockSpec(memory_space=pltpu.VMEM)
    smem = pl.BlockSpec(memory_space=pltpu.SMEM)
    hbm = pl.BlockSpec(memory_space=pltpu.HBM)
    shape = jax.ShapeDtypeStruct
    taps_lon = taps_lon.astype(bf16).astype(f32)
    taps_lat = taps_lat.astype(bf16).astype(f32)
    flat = controls.reshape(members, cells, levels)

    flank = rim * lon_tile
    low, rim1, rim2, info, *sides = pl.pallas_call(
        functools.partial(start_kernel, (rim, lon_tile, lat_tile, blocks)),
        out_shape=[shape((members * cells, levels), bf16)] + [shape((members * edge + tail, levels), bf16)] * 2
        + [shape((up8(2 * blocks), levels), f32)] + [shape((members * flank + tail, levels), bf16)] * len(lat_pairs),
        in_specs=[vmem] * 2, out_specs=[vmem] * (4 + len(lat_pairs)), compiler_params=params(),
    )(flat, obs_columns.reshape(1, n_slots))
    halos = [lax.ppermute(r, "lon", p) for r, p in zip((rim1, rim2), lon_pairs)]
    sides = [lax.ppermute(r, "lat", p) for r, p in zip(sides, lat_pairs)]
    n_tiles = 1 + len(lat_pairs)
    live = lax.broadcasted_iota(jnp.int32, (1, n_slots), 1) < obs_count[0]
    scale = jnp.where(live, 0.5 * obs_quality[0, 0].astype(f32), 0.0)
    info, scale = lax.optimization_barrier((info, scale))
    step = 1
    while step < n_mem:
        info = info + lax.ppermute(info, "mem", [(i, i ^ step) for i in range(n_mem)])
        step *= 2
    n_rims = 2 * n_tiles

    own = pl.pallas_call(
        functools.partial(pick_kernel, lat_tile, blocks),
        out_shape=shape((slots, wide), bf16),
        in_specs=[vmem] * 2, out_specs=vmem, compiler_params=params(),
    )(info, ensemble.reshape(members, cells, levels))
    base, *weights = pl.pallas_call(
        functools.partial(prep_kernel, (lon_tile, lat_tile, rim, members, blocks)),
        out_shape=[shape((slots, wide), f32)] + [shape((slots, edge), bf16)] * n_rims,
        in_specs=[smem] * 2 + [vmem] * (1 + n_tiles), out_specs=[vmem] * (1 + n_rims), compiler_params=params(),
    )(taps_lon, taps_lat, info, low, *sides)

    halos[0], own = lax.optimization_barrier((halos[0], own))
    rims = list(halos)
    for p in lat_pairs:
        rims += [lax.ppermute(h, "lat", p) for h in halos]

    tall = slots + up8(2 * blocks * (3 * n_tiles - 1) + blocks)
    tails = [t[members * flank:] for t in sides]
    mine = pl.pallas_call(
        functools.partial(part_kernel, blocks),
        out_shape=shape((tall, levels), f32),
        in_specs=[vmem] * (4 + len(tails) + 2 * len(rims)), out_specs=vmem, compiler_params=params(),
    )(base, own, obs_values.reshape(n_slots, levels), scale, *tails, *weights, *rims)
    terms = sum_terms(mine, n_mem)

    resid, send, extra = pl.pallas_call(
        functools.partial(resid_kernel, blocks, n_tiles),
        out_shape=[shape((slots, levels), f32), shape((slots, wide), bf16), shape((tall - slots, levels), f32)],
        in_specs=[vmem] * (1 + len(terms)), out_specs=[vmem] * 3, compiler_params=params(),
    )(own, *terms)

    row = [send] + [lax.ppermute(send, "lon", p) for p in lon_pairs]
    count = len(row) * n_tiles
    weight, resid = pl.pallas_call(
        functools.partial(weight_kernel, (lon_tile, lat_tile, blocks, n_tiles)),
        out_shape=[shape((cells, count * slots), bf16), shape((n_slots, levels), f32)],
        in_specs=[smem] * 2 + [vmem] * 3, out_specs=[vmem] * 2, compiler_params=params(),
    )(taps_lon, taps_lat, info, extra, resid)
    row[1], weight = lax.optimization_barrier((row[1], weight))
    around = []
    for r in row:
        around += [r] + [lax.ppermute(r, "lat", q) for q in lat_pairs]
    group = 2 if members % 2 == 0 else 1
    late = n_tiles
    begun, rest = pl.pallas_call(
        functools.partial(begin_kernel, group, edge),
        out_shape=[shape((members, cells, levels), f32), shape((members, edge, levels), f32)],
        in_specs=[vmem] * (2 + count - late), out_specs=[hbm, vmem],
        scratch_shapes=[
            pltpu.VMEM(((count - late) * slots, wide), bf16),
            pltpu.VMEM((members, cells, levels), f32),
            pltpu.SemaphoreType.DMA((members,)),
        ],
        compiler_params=params(),
    )(weight, flat, *around[:-late])
    new = pl.pallas_call(
        functools.partial(end_kernel, group),
        out_shape=shape((members, cells, levels), f32),
        in_specs=[vmem] * 2 + [hbm] + [vmem] * late, out_specs=hbm,
        scratch_shapes=[
            pltpu.VMEM((late * slots, wide), bf16),
            pltpu.VMEM((members, edge, levels), f32),
            pltpu.SemaphoreType.DMA((members,)),
        ],
        input_output_aliases={2: 0}, compiler_params=params(),
    )(weight, rest, begun, *around[-late:])
    return (new.reshape(controls.shape), resid[None, None, None])


def solution(mesh):
    placed = (
        P("mem", "lon", "lat", None),
        P("mem", "lon", "lat", None),
        P(),
        P(),
        P("lon", "lat", "mem", None),
        P("lon", "lat", "mem"),
        P("lon", "lat", "mem", None),
        P("lon", "lat", "mem", None, None),
    )
    return jax.shard_map(
        shards,
        mesh=mesh,
        in_specs=placed,
        out_specs=(P("mem", "lon", "lat", None), P("lon", "lat", "mem", None, None)),
        check_vma=False,
    )
```

```python
import functools

import jax
import jax.numpy as jnp
from jax import lax
from jax.experimental import pallas as pl
from jax.experimental.pallas import tpu as pltpu
from jax.sharding import PartitionSpec as P

descent = 0.5
f32 = jnp.float32
bf16 = jnp.bfloat16
tail = 16


def pairings(size, wraps):
    even = [(i, i ^ 1) for i in range(size)]
    odd = []
    for i in range(size):
        j = i + 1 if i % 2 else i - 1
        if wraps:
            j = j % size
        if 0 <= j < size:
            odd.append((i, j))
    return [even, odd] if odd else [even]


def sum_terms(x, count):
    if count <= 4:
        return [x] + [lax.ppermute(x, "mem", [(i, i ^ b) for i in range(count)]) for b in range(1, count)]
    step = 1
    while step < count:
        other = lax.ppermute(x, "mem", [(i, i ^ step) for i in range(count)])
        step *= 2
        if step < count:
            x = x + other
    return [x, other]


def up8(n):
    return (n + 7) // 8 * 8


def signs(axis):
    even = lax.axis_index(axis) % 2 == 0
    return [jnp.where(even, 1.0, -1.0).astype(f32), jnp.where(even, -1.0, 1.0).astype(f32)]


def fiota(shape, dim):
    return lax.broadcasted_iota(jnp.int32, shape, dim).astype(f32)


def diagonal(rows, lanes, shift=0.0):
    return fiota((rows, lanes), 0) + shift == fiota((rows, lanes), 1)


def to_rows(lanes):
    n = lanes.shape[1]
    return jnp.sum(jnp.where(diagonal(n, n), lanes, 0.0), axis=1, keepdims=True)


def to_lanes(rows):
    n = rows.shape[0]
    return jnp.sum(jnp.where(diagonal(n, n), rows, 0.0), axis=0, keepdims=True)


def owner_lanes(lanes, first, width):
    here = diagonal(lanes.shape[1], width, first.astype(f32))
    return jnp.sum(jnp.where(here, to_rows(lanes), 0.0), axis=0, keepdims=True)


def lane_row(ref, first, blocks, slots):
    if blocks == 1:
        return ref[first:first + 1, 0:slots]
    return jnp.concatenate([ref[first + r:first + r + 1, :] for r in range(blocks)], axis=1)[:, 0:slots]


def band(distance, taps_ref):
    taps = taps_ref[...].astype(bf16).astype(f32)
    out = jnp.zeros_like(distance)
    for k in range(taps.shape[1]):
        out = jnp.where(distance == float(k), taps[:, k:k + 1], out)
    return out


def dot(a, b):
    return jnp.dot(a, b, preferred_element_type=f32)


def params(mib=32):
    return pltpu.CompilerParams(vmem_limit_bytes=mib * 1024 * 1024)


def start_kernel(dims, low_ref, col_ref, rim1_ref, rim2_ref, info_ref, *refs):
    rim, lon_tile, lat_tile, blocks = dims
    side_refs, con_ref = refs[:-1], refs[-1]
    edge, cells = rim * lat_tile, lon_tile * lat_tile
    members, levels = low_ref.shape[0] // cells, low_ref.shape[1]
    n_slots = col_ref.shape[1]
    mem = lax.axis_index("mem")
    column = col_ref[...].astype(f32)
    lon_pos = jnp.floor((column + 0.5) * (1.0 / lat_tile))
    lat_pos = column - lon_pos * float(lat_tile)
    info_ref[...] = jnp.zeros_like(info_ref)
    row = lax.broadcasted_iota(jnp.int32, (tail, levels), 0)
    placed = jnp.zeros((tail, levels), f32)
    for f, lanes in enumerate((lon_pos, lat_pos)):
        for r in range(blocks):
            moved = owner_lanes(lanes, mem * n_slots - r * levels, levels)
            info_ref[f * blocks + r:f * blocks + r + 1, :] = moved
            placed = jnp.where(row == f * blocks + r, moved, placed)
    placed = placed.astype(bf16)
    even = lax.axis_index("lon") % 2 == 0
    far = cells - edge
    for at, ref in ((jnp.where(even, far, 0), rim1_ref), (jnp.where(even, 0, far), rim2_ref)):
        for m in range(members):
            ref[m * edge:(m + 1) * edge, :] = low_ref[pl.ds(pl.multiple_of(at + m * cells, 16), edge), :]
        ref[members * edge:, :] = placed
    con_ref[...] = low_ref[...].astype(f32)
    for ref, sign in zip(side_refs, signs("lat")):
        at = jnp.where(sign > 0, lat_tile - rim, 0)
        for m in range(members):
            for i in range(0, lon_tile, 2):
                pair = [con_ref[pl.ds(pl.multiple_of(at + (m * lon_tile + i + k) * lat_tile, 8), rim), :] for k in range(2)]
                row_at = (m * lon_tile + i) * rim
                ref[row_at:row_at + 2 * rim, :] = jnp.concatenate(pair, axis=0).astype(bf16)
        ref[members * lon_tile * rim:, :] = placed


def pick_kernel(lat_tile, blocks, info_ref, ens_ref, out_ref):
    members, cells, levels = ens_ref.shape
    slots = out_ref.shape[0]
    lon_pos = to_rows(lane_row(info_ref, 0, blocks, slots))
    lat_pos = to_rows(lane_row(info_ref, blocks, blocks, slots))
    cell_of = lon_pos * float(lat_tile) + lat_pos
    chosen = (fiota((slots, cells), 1) == cell_of).astype(bf16)
    for m in range(members):
        out_ref[:, m * levels:(m + 1) * levels] = dot(chosen, ens_ref[m]).astype(bf16)


def prep_kernel(dims, taps_lon, taps_lat, info_ref, low_ref, *refs):
    lon_tile, lat_tile, rim, members, blocks = dims
    count = (len(refs) - 3) // 3
    sides, base_ref, rims = refs[:count], refs[count], refs[count + 1:]
    slots, levels = base_ref.shape[0], low_ref.shape[1]
    cells, edge, flank = lon_tile * lat_tile, rim * lat_tile, rim * lon_tile
    lon_pos = to_rows(lane_row(info_ref, 0, blocks, slots))
    lat_pos = to_rows(lane_row(info_ref, blocks, blocks, slots))
    lane = fiota((slots, 128), 1)
    lon_w = band(lane - lon_pos, taps_lon).astype(bf16)
    lat_w = band(lane + float(rim - lat_tile) - lat_pos, taps_lat).astype(bf16)
    lon_side = [jnp.where(s > 0, float(lon_tile), float(-rim)) for s in signs("lon")]
    sections = [(cells, 0.0, 0.0, lat_tile)] + [(edge, o, 0.0, lat_tile) for o in lon_side]
    for s in signs("lat")[:count]:
        sections += [(edge, o, s * float(lat_tile), lat_tile) for o in lon_side]
        sections.append((flank, 0.0, jnp.where(s > 0, float(lat_tile), float(-rim)), rim))
    lon_at, lat_at = [], []
    for size, lon_off, lat_off, width in sections:
        cell = fiota((1, -(-size // 128) * 128), 1)
        lon_of = jnp.floor((cell + 0.5) * (1.0 / width))
        lon_at.append(jnp.where(cell < size, lon_of + (lon_off + float(rim)), -1.0))
        lat_at.append(cell - lon_of * float(width) + (lat_off + float(lat_tile)))
    lon_at, lat_at = jnp.concatenate(lon_at, axis=1), jnp.concatenate(lat_at, axis=1)
    place = fiota((128, lon_at.shape[1]), 0)
    lon_e = dot(lon_w[:, 0:64], (place[0:64] == lon_at).astype(bf16))
    lat_e = dot(lat_w, (place == lat_at).astype(bf16))
    weight = (lon_e * lat_e).astype(bf16)
    ends = [0]
    for size, _, _, _ in sections:
        ends.append(ends[-1] + -(-size // 128) * 128)
    pieces = [weight[:, e:e + section[0]] for e, section in zip(ends, sections)]
    for m in range(members):
        part = dot(pieces[0], low_ref[m * cells:(m + 1) * cells, :])
        for t, side in enumerate(sides):
            part += dot(pieces[3 * t + 5], side[m * flank:(m + 1) * flank, :])
        base_ref[:, m * levels:(m + 1) * levels] = part
    kept = pieces[1:3]
    for t in range(count):
        kept += pieces[3 * t + 3:3 * t + 5]
    for ref, piece in zip(rims, kept):
        ref[...] = piece


def part_kernel(blocks, base_ref, own_ref, values_ref, scale_ref, *refs):
    out_ref = refs[-1]
    count = (len(refs) + 2) // 5
    tails, weights, halos = refs[:count - 1], refs[count - 1:3 * count - 2], refs[3 * count - 2:-1]
    n_slots, levels = values_ref.shape
    slots, wide = base_ref.shape
    members = wide // levels
    block = weights[0].shape[1]
    total = jnp.zeros((slots, levels), f32)
    for m in range(members):
        lanes = slice(m * levels, (m + 1) * levels)
        spread = base_ref[:, lanes]
        for w, h in zip(weights, halos):
            spread += dot(w[...], h[m * block:(m + 1) * block, :])
        total += spread * own_ref[:, lanes].astype(f32)
    out_ref[slots:, :] = jnp.zeros((out_ref.shape[0] - slots, levels), f32)
    at = slots
    for t in range(count):
        for ref in halos[2 * t:2 * t + 2] + tails[t:t + 1]:
            rows = ref[...] if ref.shape[0] == tail else ref[members * block:, :]
            out_ref[at:at + 2 * blocks, :] = rows.astype(f32)[0:2 * blocks]
            at += 2 * blocks
    at += 2 * blocks
    mem = lax.axis_index("mem")
    for r in range(blocks):
        out_ref[at + r:at + r + 1, :] = owner_lanes(scale_ref[...], mem * n_slots - r * levels, levels)
    out_ref[0:slots, :] = total
    mine = pl.ds(pl.multiple_of(mem * n_slots, n_slots), n_slots)
    out_ref[mine, :] = out_ref[mine, :] - values_ref[...]


def last_kernel(blocks, count, part_ref, own_ref, weight_ref, halo_ref, out_ref):
    slots, block = weight_ref.shape
    levels = part_ref.shape[1]
    members = own_ref.shape[1] // levels
    total = part_ref[0:slots, :]
    for m in range(members):
        lanes = slice(m * levels, (m + 1) * levels)
        total += dot(weight_ref[...], halo_ref[m * block:(m + 1) * block, :]) * own_ref[:, lanes].astype(f32)
    out_ref[0:slots, :] = total
    out_ref[slots:, :] = part_ref[slots:, :]
    at = slots + 2 * blocks * (3 * count - 2)
    out_ref[at:at + 2 * blocks, :] = halo_ref[members * block:, :].astype(f32)[0:2 * blocks]


def resid_kernel(blocks, tiles, own_ref, *refs):
    terms, (resid_ref, send_ref, extra_ref) = refs[:-3], refs[-3:]
    slots, wide = send_ref.shape
    levels = resid_ref.shape[1]
    total = terms[0][...]
    for t in terms[1:]:
        total = total + t[...]
    extra_ref[...] = total[slots:]
    resid = to_rows(lane_row(extra_ref, 2 * blocks * (3 * tiles - 1), blocks, slots)) * total[0:slots]
    for m in range(wide // levels):
        lanes = slice(m * levels, (m + 1) * levels)
        send_ref[:, lanes] = (own_ref[:, lanes].astype(f32) * resid).astype(bf16)
    resid_ref[...] = resid


def weight_kernel(dims, taps_lon, taps_lat, info_ref, extra_ref, resid_ref, out_ref, mine_ref):
    lon_tile, lat_tile, blocks, tiles = dims
    slots, levels = resid_ref.shape
    n_slots = mine_ref.shape[0]
    mine_ref[...] = resid_ref[pl.ds(pl.multiple_of(lax.axis_index("mem") * n_slots, n_slots), n_slots), :]
    rim = taps_lon.shape[1] // 2
    lon_sign, lat_sign = signs("lon"), signs("lat")
    at = 0
    placed = []
    for t in range(tiles):
        shift = 0.0 if t == 0 else lat_sign[t - 1] * float(lat_tile)
        beside = []
        for side in range(2):
            beside.append((lane_row(extra_ref, at, blocks, slots) + lon_sign[side] * float(lon_tile), lane_row(extra_ref, at + blocks, blocks, slots)))
            at += 2 * blocks
        if t == 0:
            here = (lane_row(info_ref, 0, blocks, slots), lane_row(info_ref, blocks, blocks, slots))
        else:
            here = after
        if t + 1 < tiles:
            after = (lane_row(extra_ref, at, blocks, slots), lane_row(extra_ref, at + blocks, blocks, slots))
            at += 2 * blocks
        placed.append([(lon_at, lat_at + shift) for lon_at, lat_at in [here] + beside])
    lon_pos = [placed[t][k][0] for k in range(3) for t in range(tiles)]
    lat_pos = [placed[t][k][1] for k in range(3) for t in range(tiles)]
    lon_pos, lat_pos = jnp.concatenate(lon_pos, axis=1), jnp.concatenate(lat_pos, axis=1)
    tall = 32
    lon_w = band(fiota((tall, lon_pos.shape[1]), 0) + rim - lon_pos, taps_lon)
    lat_w = band(fiota((tall, lat_pos.shape[1]), 0) + rim - lat_pos, taps_lat)
    cells = lon_tile * lat_tile
    lon_of = fiota((lon_tile, lat_tile, tall), 0).reshape(cells, tall)
    lat_of = fiota((lon_tile, lat_tile, tall), 1).reshape(cells, tall)
    place = fiota((cells, tall), 1)
    lon_e = dot((place == lon_of).astype(bf16), lon_w.astype(bf16))
    lat_e = dot((place == lat_of).astype(bf16), lat_w.astype(bf16))
    out_ref[...] = (lon_e * lat_e).astype(bf16)


def begin_kernel(group, edge, weight_ref, con_ref, *refs):
    sets, out_hbm, rest_ref, all_ref, buf, sem = refs[:-5], refs[-5], refs[-4], refs[-3], refs[-2], refs[-1]
    members, cells, levels = con_ref.shape
    slots = sets[0].shape[0]
    for s, ref in enumerate(sets):
        all_ref[s * slots:(s + 1) * slots, :] = ref[...]
    depth = len(sets) * slots
    last = signs("lon")[1] > 0
    done = pl.ds(pl.multiple_of(jnp.where(last, 0, edge), 16), cells - edge)
    left = pl.ds(pl.multiple_of(jnp.where(last, cells - edge, 0), 16), edge)
    copies = []
    for m in range(0, members, group):
        back = dot(weight_ref[:, 0:depth], all_ref[:, m * levels:(m + group) * levels])
        for k in range(group):
            con = con_ref[m + k]
            buf[m + k] = con - descent * (con + back[:, k * levels:(k + 1) * levels])
            copies.append(pltpu.make_async_copy(buf.at[m + k, done], out_hbm.at[m + k, done], sem.at[m + k]))
            copies[-1].start()
    for m in range(members):
        rest_ref[m] = buf[m, left, :]
    for copy in copies:
        copy.wait()


def end_kernel(group, weight_ref, rest_ref, begun_hbm, *refs):
    sets, out_hbm, all_ref, buf, sem = refs[:-4], refs[-4], refs[-3], refs[-2], refs[-1]
    members, edge, levels = rest_ref.shape
    cells = weight_ref.shape[0]
    slots = sets[0].shape[0]
    for s, ref in enumerate(sets):
        all_ref[s * slots:(s + 1) * slots, :] = ref[...]
    begin = weight_ref.shape[1] - len(sets) * slots
    left = pl.ds(pl.multiple_of(jnp.where(signs("lon")[1] > 0, cells - edge, 0), 16), edge)
    weight = weight_ref[left, begin:]
    copies = []
    for m in range(0, members, group):
        back = dot(weight, all_ref[:, m * levels:(m + group) * levels])
        for k in range(group):
            buf[m + k] = rest_ref[m + k] - descent * back[:, k * levels:(k + 1) * levels]
            copies.append(pltpu.make_async_copy(buf.at[m + k], out_hbm.at[m + k, left], sem.at[m + k]))
            copies[-1].start()
    for copy in copies:
        copy.wait()


def shards(controls, ensemble, taps_lon, taps_lat, obs_columns, obs_count, obs_quality, obs_values):
    rim = taps_lon.shape[0] // 2
    members, lon_tile, lat_tile, levels = controls.shape
    n_slots = obs_columns.shape[-1]
    n_mem = lax.axis_size("mem")
    slots = n_slots * n_mem
    blocks = (slots + levels - 1) // levels
    cells = lon_tile * lat_tile
    edge = rim * lat_tile
    wide = members * levels
    lon_pairs = pairings(lax.axis_size("lon"), True)
    lat_pairs = pairings(lax.axis_size("lat"), False)
    vmem = pl.BlockSpec(memory_space=pltpu.VMEM)
    hbm = pl.BlockSpec(memory_space=pltpu.HBM)
    shape = jax.ShapeDtypeStruct
    taps_lon, taps_lat = taps_lon.reshape(1, -1), taps_lat.reshape(1, -1)
    flat = controls.reshape(members, cells, levels)

    flank = rim * lon_tile
    low = controls.astype(bf16).reshape(members * cells, levels)
    rim1, rim2, info, *sides = pl.pallas_call(
        functools.partial(start_kernel, (rim, lon_tile, lat_tile, blocks)),
        out_shape=[shape((members * edge + tail, levels), bf16)] * 2 + [shape((up8(2 * blocks), levels), f32)]
        + [shape((members * flank + tail, levels), bf16)] * len(lat_pairs),
        in_specs=[vmem] * 2, out_specs=[vmem] * (3 + len(lat_pairs)),
        scratch_shapes=[pltpu.VMEM((members * cells, levels), f32)], compiler_params=params(),
    )(low, obs_columns.reshape(1, n_slots))
    halos = [lax.ppermute(r, "lon", p) for r, p in zip((rim1, rim2), lon_pairs)]
    sides = [lax.ppermute(r, "lat", p) for r, p in zip(sides, lat_pairs)]
    n_tiles = 1 + len(lat_pairs)
    live = lax.broadcasted_iota(jnp.int32, (1, n_slots), 1) < obs_count[0]
    scale = jnp.where(live, 0.5 * obs_quality[0, 0].astype(f32), 0.0)
    info, scale = lax.optimization_barrier((info, scale))
    step = 1
    while step < n_mem:
        info = info + lax.ppermute(info, "mem", [(i, i ^ step) for i in range(n_mem)])
        step *= 2
    n_rims = 2 * n_tiles

    own = pl.pallas_call(
        functools.partial(pick_kernel, lat_tile, blocks),
        out_shape=shape((slots, wide), bf16),
        in_specs=[vmem] * 2, out_specs=vmem, compiler_params=params(),
    )(info, ensemble.reshape(members, cells, levels))
    base, *weights = pl.pallas_call(
        functools.partial(prep_kernel, (lon_tile, lat_tile, rim, members, blocks)),
        out_shape=[shape((slots, wide), f32)] + [shape((slots, edge), bf16)] * n_rims,
        in_specs=[vmem] * (3 + n_tiles), out_specs=[vmem] * (1 + n_rims), compiler_params=params(),
    )(taps_lon, taps_lat, info, low, *sides)

    halos[0], own = lax.optimization_barrier((halos[0], own))
    rims = list(halos)
    for p in lat_pairs:
        rims += [lax.ppermute(h, "lat", p) for h in halos]

    tall = slots + up8(2 * blocks * (3 * n_tiles - 1) + blocks)
    tails = [t[members * flank:] for t in sides]
    part = pl.pallas_call(
        functools.partial(part_kernel, blocks),
        out_shape=shape((tall, levels), f32),
        in_specs=[vmem] * (2 + len(tails) + 2 * len(rims)), out_specs=vmem, compiler_params=params(),
    )(base, own, obs_values.reshape(n_slots, levels), scale, *tails, *weights[:-1], *rims[:-1])
    mine = pl.pallas_call(
        functools.partial(last_kernel, blocks, n_tiles),
        out_shape=shape((tall, levels), f32),
        in_specs=[vmem] * 4, out_specs=vmem, compiler_params=params(),
    )(part, own, weights[-1], rims[-1])
    terms = sum_terms(mine, n_mem)

    resid, send, extra = pl.pallas_call(
        functools.partial(resid_kernel, blocks, n_tiles),
        out_shape=[shape((slots, levels), f32), shape((slots, wide), bf16), shape((tall - slots, levels), f32)],
        in_specs=[vmem] * (1 + len(terms)), out_specs=[vmem] * 3, compiler_params=params(),
    )(own, *terms)

    row = [send] + [lax.ppermute(send, "lon", p) for p in lon_pairs]
    count = len(row) * n_tiles
    weight, resid = pl.pallas_call(
        functools.partial(weight_kernel, (lon_tile, lat_tile, blocks, n_tiles)),
        out_shape=[shape((cells, count * slots), bf16), shape((n_slots, levels), f32)],
        in_specs=[vmem] * 5, out_specs=[vmem] * 2, compiler_params=params(),
    )(taps_lon, taps_lat, info, extra, resid)
    row[1], weight = lax.optimization_barrier((row[1], weight))
    around = []
    for r in row:
        around += [r] + [lax.ppermute(r, "lat", q) for q in lat_pairs]
    group = 2 if members % 2 == 0 else 1
    late = n_tiles
    begun, rest = pl.pallas_call(
        functools.partial(begin_kernel, group, edge),
        out_shape=[shape((members, cells, levels), f32), shape((members, edge, levels), f32)],
        in_specs=[vmem] * (2 + count - late), out_specs=[hbm, vmem],
        scratch_shapes=[
            pltpu.VMEM(((count - late) * slots, wide), bf16),
            pltpu.VMEM((members, cells, levels), f32),
            pltpu.SemaphoreType.DMA((members,)),
        ],
        compiler_params=params(),
    )(weight, flat, *around[:-late])
    new = pl.pallas_call(
        functools.partial(end_kernel, group),
        out_shape=shape((members, cells, levels), f32),
        in_specs=[vmem] * 2 + [hbm] + [vmem] * late, out_specs=hbm,
        scratch_shapes=[
            pltpu.VMEM((late * slots, wide), bf16),
            pltpu.VMEM((members, edge, levels), f32),
            pltpu.SemaphoreType.DMA((members,)),
        ],
        input_output_aliases={2: 0}, compiler_params=params(),
    )(weight, rest, begun, *around[-late:])
    return (new.reshape(controls.shape), resid[None, None, None])


def solution(mesh):
    placed = (
        P("mem", "lon", "lat", None),
        P("mem", "lon", "lat", None),
        P(),
        P(),
        P("lon", "lat", "mem", None),
        P("lon", "lat", "mem"),
        P("lon", "lat", "mem", None),
        P("lon", "lat", "mem", None, None),
    )
    return jax.shard_map(
        shards,
        mesh=mesh,
        in_specs=placed,
        out_specs=(P("mem", "lon", "lat", None), P("lon", "lat", "mem", None, None)),
        check_vma=False,
    )
```

```python
import functools

import jax
import jax.numpy as jnp
from jax import lax
from jax.experimental import pallas as pl
from jax.experimental.pallas import tpu as pltpu
from jax.sharding import PartitionSpec as P

descent = 0.5
f32 = jnp.float32
bf16 = jnp.bfloat16
tail = 16


def pairings(size, wraps):
    even = [(i, i ^ 1) for i in range(size)]
    odd = []
    for i in range(size):
        j = i + 1 if i % 2 else i - 1
        if wraps:
            j = j % size
        if 0 <= j < size:
            odd.append((i, j))
    return [even, odd] if odd else [even]


def sum_terms(x, count):
    if count <= 4:
        return [x] + [lax.ppermute(x, "mem", [(i, i ^ b) for i in range(count)]) for b in range(1, count)]
    step = 1
    while step < count:
        other = lax.ppermute(x, "mem", [(i, i ^ step) for i in range(count)])
        step *= 2
        if step < count:
            x = x + other
    return [x, other]


def up8(n):
    return (n + 7) // 8 * 8


def signs(axis):
    even = lax.axis_index(axis) % 2 == 0
    return [jnp.where(even, 1.0, -1.0).astype(f32), jnp.where(even, -1.0, 1.0).astype(f32)]


def fiota(shape, dim):
    return lax.broadcasted_iota(jnp.int32, shape, dim).astype(f32)


def diagonal(rows, lanes, shift=0.0):
    return fiota((rows, lanes), 0) + shift == fiota((rows, lanes), 1)


def to_rows(lanes):
    n = lanes.shape[1]
    return jnp.sum(jnp.where(diagonal(n, n), lanes, 0.0), axis=1, keepdims=True)


def to_lanes(rows):
    n = rows.shape[0]
    return jnp.sum(jnp.where(diagonal(n, n), rows, 0.0), axis=0, keepdims=True)


def owner_lanes(lanes, first, width):
    here = diagonal(lanes.shape[1], width, first.astype(f32))
    return jnp.sum(jnp.where(here, to_rows(lanes), 0.0), axis=0, keepdims=True)


def lane_row(ref, first, blocks, slots):
    if blocks == 1:
        return ref[first:first + 1, 0:slots]
    return jnp.concatenate([ref[first + r:first + r + 1, :] for r in range(blocks)], axis=1)[:, 0:slots]


def band(distance, taps_ref):
    taps = taps_ref[...].astype(bf16).astype(f32)
    out = jnp.zeros_like(distance)
    for k in range(taps.shape[1]):
        out = jnp.where(distance == float(k), taps[:, k:k + 1], out)
    return out


def dot(a, b):
    return jnp.dot(a, b, preferred_element_type=f32)


def params(mib=32):
    return pltpu.CompilerParams(vmem_limit_bytes=mib * 1024 * 1024)


def start_kernel(dims, first_ref, last_ref, col_ref, rim1_ref, rim2_ref, info_ref):
    lat_tile, blocks = dims
    edge, levels = first_ref.shape
    n_slots = col_ref.shape[1]
    mem = lax.axis_index("mem")
    column = col_ref[...].astype(f32)
    lon_pos = jnp.floor((column + 0.5) * (1.0 / lat_tile))
    lat_pos = column - lon_pos * float(lat_tile)
    info_ref[...] = jnp.zeros_like(info_ref)
    row = lax.broadcasted_iota(jnp.int32, (tail, levels), 0)
    placed = jnp.zeros((tail, levels), f32)
    for f, lanes in enumerate((lon_pos, lat_pos)):
        for r in range(blocks):
            moved = owner_lanes(lanes, mem * n_slots - r * levels, levels)
            info_ref[f * blocks + r:f * blocks + r + 1, :] = moved
            placed = jnp.where(row == f * blocks + r, moved, placed)
    even = lax.axis_index("lon") % 2 == 0

    @pl.when(even)
    def _():
        rim1_ref[0:edge, :] = last_ref[...].astype(bf16)
        rim2_ref[0:edge, :] = first_ref[...].astype(bf16)

    @pl.when(jnp.logical_not(even))
    def _():
        rim1_ref[0:edge, :] = first_ref[...].astype(bf16)
        rim2_ref[0:edge, :] = last_ref[...].astype(bf16)

    for ref in (rim1_ref, rim2_ref):
        ref[edge:, :] = placed.astype(bf16)


def low_kernel(dims, con_ref, info_ref, low_ref, *side_refs):
    rim, lon_tile, lat_tile, blocks = dims
    members, cells, levels = con_ref.shape
    row = lax.broadcasted_iota(jnp.int32, (tail, levels), 0)
    placed = jnp.zeros((tail, levels), f32)
    for r in range(2 * blocks):
        placed = jnp.where(row == r, info_ref[r:r + 1, :], placed)
    for ref, sign in zip(side_refs, signs("lat")):
        at = jnp.where(sign > 0, lat_tile - rim, 0)
        for m in range(members):
            for i in range(0, lon_tile, 2):
                pair = [con_ref[m, pl.ds(pl.multiple_of(at + (i + k) * lat_tile, 8), rim), :] for k in range(2)]
                row_at = (m * lon_tile + i) * rim
                ref[row_at:row_at + 2 * rim, :] = jnp.concatenate(pair, axis=0).astype(bf16)
        ref[members * lon_tile * rim:, :] = placed.astype(bf16)
    for m in range(members):
        low_ref[m * cells:(m + 1) * cells, :] = con_ref[m].astype(bf16)


def pick_kernel(lat_tile, blocks, info_ref, ens_ref, out_ref):
    members, cells, levels = ens_ref.shape
    slots = out_ref.shape[0]
    lon_pos = to_rows(lane_row(info_ref, 0, blocks, slots))
    lat_pos = to_rows(lane_row(info_ref, blocks, blocks, slots))
    cell_of = lon_pos * float(lat_tile) + lat_pos
    chosen = (fiota((slots, cells), 1) == cell_of).astype(bf16)
    for m in range(members):
        out_ref[:, m * levels:(m + 1) * levels] = dot(chosen, ens_ref[m]).astype(bf16)


def prep_kernel(dims, taps_lon, taps_lat, info_ref, low_ref, *refs):
    lon_tile, lat_tile, rim, members, blocks = dims
    count = (len(refs) - 3) // 3
    sides, base_ref, rims = refs[:count], refs[count], refs[count + 1:]
    slots, levels = base_ref.shape[0], low_ref.shape[1]
    cells, edge, flank = lon_tile * lat_tile, rim * lat_tile, rim * lon_tile
    lon_pos = to_rows(lane_row(info_ref, 0, blocks, slots))
    lat_pos = to_rows(lane_row(info_ref, blocks, blocks, slots))
    lane = fiota((slots, 128), 1)
    lon_w = band(lane - lon_pos, taps_lon).astype(bf16)
    lat_w = band(lane + float(rim - lat_tile) - lat_pos, taps_lat).astype(bf16)
    lon_side = [jnp.where(s > 0, float(lon_tile), float(-rim)) for s in signs("lon")]
    sections = [(cells, 0.0, 0.0, lat_tile)] + [(edge, o, 0.0, lat_tile) for o in lon_side]
    for s in signs("lat")[:count]:
        sections += [(edge, o, s * float(lat_tile), lat_tile) for o in lon_side]
        sections.append((flank, 0.0, jnp.where(s > 0, float(lat_tile), float(-rim)), rim))
    lon_at, lat_at = [], []
    for size, lon_off, lat_off, width in sections:
        cell = fiota((1, -(-size // 128) * 128), 1)
        lon_of = jnp.floor((cell + 0.5) * (1.0 / width))
        lon_at.append(jnp.where(cell < size, lon_of + (lon_off + float(rim)), -1.0))
        lat_at.append(cell - lon_of * float(width) + (lat_off + float(lat_tile)))
    lon_at, lat_at = jnp.concatenate(lon_at, axis=1), jnp.concatenate(lat_at, axis=1)
    place = fiota((128, lon_at.shape[1]), 0)
    lon_e = dot(lon_w[:, 0:64], (place[0:64] == lon_at).astype(bf16))
    lat_e = dot(lat_w, (place == lat_at).astype(bf16))
    weight = (lon_e * lat_e).astype(bf16)
    ends = [0]
    for size, _, _, _ in sections:
        ends.append(ends[-1] + -(-size // 128) * 128)
    pieces = [weight[:, e:e + section[0]] for e, section in zip(ends, sections)]
    for m in range(members):
        part = dot(pieces[0], low_ref[m * cells:(m + 1) * cells, :])
        for t, side in enumerate(sides):
            part += dot(pieces[3 * t + 5], side[m * flank:(m + 1) * flank, :])
        base_ref[:, m * levels:(m + 1) * levels] = part
    kept = pieces[1:3]
    for t in range(count):
        kept += pieces[3 * t + 3:3 * t + 5]
    for ref, piece in zip(rims, kept):
        ref[...] = piece


def part_kernel(blocks, base_ref, own_ref, values_ref, scale_ref, *refs):
    out_ref = refs[-1]
    count = (len(refs) + 2) // 5
    tails, weights, halos = refs[:count - 1], refs[count - 1:3 * count - 2], refs[3 * count - 2:-1]
    n_slots, levels = values_ref.shape
    slots, wide = base_ref.shape
    members = wide // levels
    block = weights[0].shape[1]
    total = jnp.zeros((slots, levels), f32)
    for m in range(members):
        lanes = slice(m * levels, (m + 1) * levels)
        spread = base_ref[:, lanes]
        for w, h in zip(weights, halos):
            spread += dot(w[...], h[m * block:(m + 1) * block, :])
        total += spread * own_ref[:, lanes].astype(f32)
    out_ref[slots:, :] = jnp.zeros((out_ref.shape[0] - slots, levels), f32)
    at = slots
    for t in range(count):
        for ref in halos[2 * t:2 * t + 2] + tails[t:t + 1]:
            rows = ref[...] if ref.shape[0] == tail else ref[members * block:, :]
            out_ref[at:at + 2 * blocks, :] = rows.astype(f32)[0:2 * blocks]
            at += 2 * blocks
    at += 2 * blocks
    mem = lax.axis_index("mem")
    for r in range(blocks):
        out_ref[at + r:at + r + 1, :] = owner_lanes(scale_ref[...], mem * n_slots - r * levels, levels)
    out_ref[0:slots, :] = total
    mine = pl.ds(pl.multiple_of(mem * n_slots, n_slots), n_slots)
    out_ref[mine, :] = out_ref[mine, :] - values_ref[...]


def last_kernel(blocks, count, part_ref, own_ref, weight_ref, halo_ref, out_ref):
    slots, block = weight_ref.shape
    levels = part_ref.shape[1]
    members = own_ref.shape[1] // levels
    total = part_ref[0:slots, :]
    for m in range(members):
        lanes = slice(m * levels, (m + 1) * levels)
        total += dot(weight_ref[...], halo_ref[m * block:(m + 1) * block, :]) * own_ref[:, lanes].astype(f32)
    out_ref[0:slots, :] = total
    out_ref[slots:, :] = part_ref[slots:, :]
    at = slots + 2 * blocks * (3 * count - 2)
    out_ref[at:at + 2 * blocks, :] = halo_ref[members * block:, :].astype(f32)[0:2 * blocks]


def resid_kernel(blocks, tiles, own_ref, *refs):
    terms, (resid_ref, send_ref, extra_ref) = refs[:-3], refs[-3:]
    slots, wide = send_ref.shape
    levels = resid_ref.shape[1]
    total = terms[0][...]
    for t in terms[1:]:
        total = total + t[...]
    extra_ref[...] = total[slots:]
    resid = to_rows(lane_row(extra_ref, 2 * blocks * (3 * tiles - 1), blocks, slots)) * total[0:slots]
    for m in range(wide // levels):
        lanes = slice(m * levels, (m + 1) * levels)
        send_ref[:, lanes] = (own_ref[:, lanes].astype(f32) * resid).astype(bf16)
    resid_ref[...] = resid


def weight_kernel(dims, taps_lon, taps_lat, info_ref, extra_ref, resid_ref, out_ref, mine_ref):
    lon_tile, lat_tile, blocks, tiles = dims
    slots, levels = resid_ref.shape
    n_slots = mine_ref.shape[0]
    mine_ref[...] = resid_ref[pl.ds(pl.multiple_of(lax.axis_index("mem") * n_slots, n_slots), n_slots), :]
    rim = taps_lon.shape[1] // 2
    lon_sign, lat_sign = signs("lon"), signs("lat")
    at = 0
    placed = []
    for t in range(tiles):
        shift = 0.0 if t == 0 else lat_sign[t - 1] * float(lat_tile)
        beside = []
        for side in range(2):
            beside.append((lane_row(extra_ref, at, blocks, slots) + lon_sign[side] * float(lon_tile), lane_row(extra_ref, at + blocks, blocks, slots)))
            at += 2 * blocks
        if t == 0:
            here = (lane_row(info_ref, 0, blocks, slots), lane_row(info_ref, blocks, blocks, slots))
        else:
            here = after
        if t + 1 < tiles:
            after = (lane_row(extra_ref, at, blocks, slots), lane_row(extra_ref, at + blocks, blocks, slots))
            at += 2 * blocks
        placed.append([(lon_at, lat_at + shift) for lon_at, lat_at in [here] + beside])
    lon_pos = [placed[t][k][0] for k in range(3) for t in range(tiles)]
    lat_pos = [placed[t][k][1] for k in range(3) for t in range(tiles)]
    lon_pos, lat_pos = jnp.concatenate(lon_pos, axis=1), jnp.concatenate(lat_pos, axis=1)
    tall = 32
    lon_w = band(fiota((tall, lon_pos.shape[1]), 0) + rim - lon_pos, taps_lon)
    lat_w = band(fiota((tall, lat_pos.shape[1]), 0) + rim - lat_pos, taps_lat)
    cells = lon_tile * lat_tile
    lon_of = fiota((lon_tile, lat_tile, tall), 0).reshape(cells, tall)
    lat_of = fiota((lon_tile, lat_tile, tall), 1).reshape(cells, tall)
    place = fiota((cells, tall), 1)
    lon_e = dot((place == lon_of).astype(bf16), lon_w.astype(bf16))
    lat_e = dot((place == lat_of).astype(bf16), lat_w.astype(bf16))
    out_ref[...] = (lon_e * lat_e).astype(bf16)


def begin_kernel(group, edge, weight_ref, con_ref, *refs):
    sets, out_hbm, rest_ref, all_ref, buf, sem = refs[:-5], refs[-5], refs[-4], refs[-3], refs[-2], refs[-1]
    members, cells, levels = con_ref.shape
    slots = sets[0].shape[0]
    for s, ref in enumerate(sets):
        all_ref[s * slots:(s + 1) * slots, :] = ref[...]
    depth = len(sets) * slots
    last = signs("lon")[1] > 0
    done = pl.ds(pl.multiple_of(jnp.where(last, 0, edge), 16), cells - edge)
    left = pl.ds(pl.multiple_of(jnp.where(last, cells - edge, 0), 16), edge)
    copies = []
    for m in range(0, members, group):
        back = dot(weight_ref[:, 0:depth], all_ref[:, m * levels:(m + group) * levels])
        for k in range(group):
            con = con_ref[m + k]
            buf[m + k] = con - descent * (con + back[:, k * levels:(k + 1) * levels])
            copies.append(pltpu.make_async_copy(buf.at[m + k, done], out_hbm.at[m + k, done], sem.at[m + k]))
            copies[-1].start()
    for m in range(members):
        rest_ref[m] = buf[m, left, :]
    for copy in copies:
        copy.wait()


def end_kernel(group, weight_ref, rest_ref, begun_hbm, *refs):
    sets, out_hbm, all_ref, buf, sem = refs[:-4], refs[-4], refs[-3], refs[-2], refs[-1]
    members, edge, levels = rest_ref.shape
    cells = weight_ref.shape[0]
    slots = sets[0].shape[0]
    for s, ref in enumerate(sets):
        all_ref[s * slots:(s + 1) * slots, :] = ref[...]
    begin = weight_ref.shape[1] - len(sets) * slots
    left = pl.ds(pl.multiple_of(jnp.where(signs("lon")[1] > 0, cells - edge, 0), 16), edge)
    weight = weight_ref[left, begin:]
    copies = []
    for m in range(0, members, group):
        back = dot(weight, all_ref[:, m * levels:(m + group) * levels])
        for k in range(group):
            buf[m + k] = rest_ref[m + k] - descent * back[:, k * levels:(k + 1) * levels]
            copies.append(pltpu.make_async_copy(buf.at[m + k], out_hbm.at[m + k, left], sem.at[m + k]))
            copies[-1].start()
    for copy in copies:
        copy.wait()


def shards(controls, ensemble, taps_lon, taps_lat, obs_columns, obs_count, obs_quality, obs_values):
    rim = taps_lon.shape[0] // 2
    members, lon_tile, lat_tile, levels = controls.shape
    n_slots = obs_columns.shape[-1]
    n_mem = lax.axis_size("mem")
    slots = n_slots * n_mem
    blocks = (slots + levels - 1) // levels
    cells = lon_tile * lat_tile
    edge = rim * lat_tile
    wide = members * levels
    lon_pairs = pairings(lax.axis_size("lon"), True)
    lat_pairs = pairings(lax.axis_size("lat"), False)
    vmem = pl.BlockSpec(memory_space=pltpu.VMEM)
    hbm = pl.BlockSpec(memory_space=pltpu.HBM)
    shape = jax.ShapeDtypeStruct
    taps_lon, taps_lat = taps_lon.reshape(1, -1), taps_lat.reshape(1, -1)
    flat = controls.reshape(members, cells, levels)

    flank = rim * lon_tile
    first = controls[:, :rim].reshape(members * edge, levels)
    last = controls[:, lon_tile - rim:].reshape(members * edge, levels)
    rim1, rim2, info = pl.pallas_call(
        functools.partial(start_kernel, (lat_tile, blocks)),
        out_shape=[shape((members * edge + tail, levels), bf16)] * 2 + [shape((up8(2 * blocks), levels), f32)],
        in_specs=[vmem] * 3, out_specs=[vmem] * 3, compiler_params=params(),
    )(first, last, obs_columns.reshape(1, n_slots))
    low, *sides = pl.pallas_call(
        functools.partial(low_kernel, (rim, lon_tile, lat_tile, blocks)),
        out_shape=[shape((members * cells, levels), bf16)] + [shape((members * flank + tail, levels), bf16)] * len(lat_pairs),
        in_specs=[vmem] * 2, out_specs=[vmem] * (1 + len(lat_pairs)), compiler_params=params(),
    )(flat, info)
    halos = [lax.ppermute(r, "lon", p) for r, p in zip((rim1, rim2), lon_pairs)]
    sides = [lax.ppermute(r, "lat", p) for r, p in zip(sides, lat_pairs)]
    n_tiles = 1 + len(lat_pairs)
    live = lax.broadcasted_iota(jnp.int32, (1, n_slots), 1) < obs_count[0]
    scale = jnp.where(live, 0.5 * obs_quality[0, 0].astype(f32), 0.0)
    info, scale = lax.optimization_barrier((info, scale))
    step = 1
    while step < n_mem:
        info = info + lax.ppermute(info, "mem", [(i, i ^ step) for i in range(n_mem)])
        step *= 2
    n_rims = 2 * n_tiles

    own = pl.pallas_call(
        functools.partial(pick_kernel, lat_tile, blocks),
        out_shape=shape((slots, wide), bf16),
        in_specs=[vmem] * 2, out_specs=vmem, compiler_params=params(),
    )(info, ensemble.reshape(members, cells, levels))
    base, *weights = pl.pallas_call(
        functools.partial(prep_kernel, (lon_tile, lat_tile, rim, members, blocks)),
        out_shape=[shape((slots, wide), f32)] + [shape((slots, edge), bf16)] * n_rims,
        in_specs=[vmem] * (3 + n_tiles), out_specs=[vmem] * (1 + n_rims), compiler_params=params(),
    )(taps_lon, taps_lat, info, low, *sides)

    halos[0], own = lax.optimization_barrier((halos[0], own))
    rims = list(halos)
    for p in lat_pairs:
        rims += [lax.ppermute(h, "lat", p) for h in halos]

    tall = slots + up8(2 * blocks * (3 * n_tiles - 1) + blocks)
    tails = [t[members * flank:] for t in sides]
    part = pl.pallas_call(
        functools.partial(part_kernel, blocks),
        out_shape=shape((tall, levels), f32),
        in_specs=[vmem] * (2 + len(tails) + 2 * len(rims)), out_specs=vmem, compiler_params=params(),
    )(base, own, obs_values.reshape(n_slots, levels), scale, *tails, *weights[:-1], *rims[:-1])
    mine = pl.pallas_call(
        functools.partial(last_kernel, blocks, n_tiles),
        out_shape=shape((tall, levels), f32),
        in_specs=[vmem] * 4, out_specs=vmem, compiler_params=params(),
    )(part, own, weights[-1], rims[-1])
    terms = sum_terms(mine, n_mem)

    resid, send, extra = pl.pallas_call(
        functools.partial(resid_kernel, blocks, n_tiles),
        out_shape=[shape((slots, levels), f32), shape((slots, wide), bf16), shape((tall - slots, levels), f32)],
        in_specs=[vmem] * (1 + len(terms)), out_specs=[vmem] * 3, compiler_params=params(),
    )(own, *terms)

    row = [send] + [lax.ppermute(send, "lon", p) for p in lon_pairs]
    count = len(row) * n_tiles
    weight, resid = pl.pallas_call(
        functools.partial(weight_kernel, (lon_tile, lat_tile, blocks, n_tiles)),
        out_shape=[shape((cells, count * slots), bf16), shape((n_slots, levels), f32)],
        in_specs=[vmem] * 5, out_specs=[vmem] * 2, compiler_params=params(),
    )(taps_lon, taps_lat, info, extra, resid)
    row[1], weight = lax.optimization_barrier((row[1], weight))
    around = []
    for r in row:
        around += [r] + [lax.ppermute(r, "lat", q) for q in lat_pairs]
    group = 2 if members % 2 == 0 else 1
    late = n_tiles
    begun, rest = pl.pallas_call(
        functools.partial(begin_kernel, group, edge),
        out_shape=[shape((members, cells, levels), f32), shape((members, edge, levels), f32)],
        in_specs=[vmem] * (2 + count - late), out_specs=[hbm, vmem],
        scratch_shapes=[
            pltpu.VMEM(((count - late) * slots, wide), bf16),
            pltpu.VMEM((members, cells, levels), f32),
            pltpu.SemaphoreType.DMA((members,)),
        ],
        compiler_params=params(),
    )(weight, flat, *around[:-late])
    new = pl.pallas_call(
        functools.partial(end_kernel, group),
        out_shape=shape((members, cells, levels), f32),
        in_specs=[vmem] * 2 + [hbm] + [vmem] * late, out_specs=hbm,
        scratch_shapes=[
            pltpu.VMEM((late * slots, wide), bf16),
            pltpu.VMEM((members, edge, levels), f32),
            pltpu.SemaphoreType.DMA((members,)),
        ],
        input_output_aliases={2: 0}, compiler_params=params(),
    )(weight, rest, begun, *around[-late:])
    return (new.reshape(controls.shape), resid[None, None, None])


def solution(mesh):
    placed = (
        P("mem", "lon", "lat", None),
        P("mem", "lon", "lat", None),
        P(),
        P(),
        P("lon", "lat", "mem", None),
        P("lon", "lat", "mem"),
        P("lon", "lat", "mem", None),
        P("lon", "lat", "mem", None, None),
    )
    return jax.shard_map(
        shards,
        mesh=mesh,
        in_specs=placed,
        out_specs=(P("mem", "lon", "lat", None), P("lon", "lat", "mem", None, None)),
        check_vma=False,
    )
```

```python
import functools

import jax
import jax.numpy as jnp
from jax import lax
from jax.experimental import pallas as pl
from jax.experimental.pallas import tpu as pltpu
from jax.sharding import PartitionSpec as P

descent = 0.5
f32 = jnp.float32
bf16 = jnp.bfloat16
tail = 16


def pairings(size, wraps):
    even = [(i, i ^ 1) for i in range(size)]
    odd = []
    for i in range(size):
        j = i + 1 if i % 2 else i - 1
        if wraps:
            j = j % size
        if 0 <= j < size:
            odd.append((i, j))
    return [even, odd] if odd else [even]


def sum_terms(x, sent, count):
    if count <= 4:
        return [x] + [lax.ppermute(sent, "mem", [(i, i ^ b) for i in range(count)]) for b in range(1, count)]
    step = 1
    while step < count:
        other = lax.ppermute(sent, "mem", [(i, i ^ step) for i in range(count)])
        step *= 2
        if step < count:
            x = x + other.astype(f32)
            sent = x.astype(bf16)
    return [x, other]


def up8(n):
    return (n + 7) // 8 * 8


def signs(axis):
    even = lax.axis_index(axis) % 2 == 0
    return [jnp.where(even, 1.0, -1.0).astype(f32), jnp.where(even, -1.0, 1.0).astype(f32)]


def fiota(shape, dim):
    return lax.broadcasted_iota(jnp.int32, shape, dim).astype(f32)


def diagonal(rows, lanes, shift=0.0):
    return fiota((rows, lanes), 0) + shift == fiota((rows, lanes), 1)


def to_rows(lanes):
    n = lanes.shape[1]
    return jnp.sum(jnp.where(diagonal(n, n), lanes, 0.0), axis=1, keepdims=True)


def to_lanes(rows):
    n = rows.shape[0]
    return jnp.sum(jnp.where(diagonal(n, n), rows, 0.0), axis=0, keepdims=True)


def owner_lanes(lanes, first, width):
    here = diagonal(lanes.shape[1], width, first.astype(f32))
    return jnp.sum(jnp.where(here, to_rows(lanes), 0.0), axis=0, keepdims=True)


def lane_row(ref, first, blocks, slots):
    if blocks == 1:
        return ref[first:first + 1, 0:slots]
    return jnp.concatenate([ref[first + r:first + r + 1, :] for r in range(blocks)], axis=1)[:, 0:slots]


def band(distance, taps_ref):
    taps = taps_ref[...].astype(bf16).astype(f32)
    out = jnp.zeros_like(distance)
    for k in range(taps.shape[1]):
        out = jnp.where(distance == float(k), taps[:, k:k + 1], out)
    return out


def dot(a, b):
    return jnp.dot(a, b, preferred_element_type=f32)


def params(mib=32):
    return pltpu.CompilerParams(vmem_limit_bytes=mib * 1024 * 1024)


def start_kernel(dims, first_ref, last_ref, col_ref, rim1_ref, rim2_ref, info_ref):
    lat_tile, blocks = dims
    edge, levels = first_ref.shape
    n_slots = col_ref.shape[1]
    mem = lax.axis_index("mem")
    column = col_ref[...].astype(f32)
    lon_pos = jnp.floor((column + 0.5) * (1.0 / lat_tile))
    lat_pos = column - lon_pos * float(lat_tile)
    info_ref[...] = jnp.zeros_like(info_ref)
    row = lax.broadcasted_iota(jnp.int32, (tail, levels), 0)
    placed = jnp.zeros((tail, levels), f32)
    for f, lanes in enumerate((lon_pos, lat_pos)):
        for r in range(blocks):
            moved = owner_lanes(lanes, mem * n_slots - r * levels, levels)
            info_ref[f * blocks + r:f * blocks + r + 1, :] = moved
            placed = jnp.where(row == f * blocks + r, moved, placed)
    even = lax.axis_index("lon") % 2 == 0

    @pl.when(even)
    def _():
        rim1_ref[0:edge, :] = last_ref[...].astype(bf16)
        rim2_ref[0:edge, :] = first_ref[...].astype(bf16)

    @pl.when(jnp.logical_not(even))
    def _():
        rim1_ref[0:edge, :] = first_ref[...].astype(bf16)
        rim2_ref[0:edge, :] = last_ref[...].astype(bf16)

    for ref in (rim1_ref, rim2_ref):
        ref[edge:, :] = placed.astype(bf16)


def low_kernel(dims, con_ref, info_ref, low_ref, *side_refs):
    rim, lon_tile, lat_tile, blocks = dims
    members, cells, levels = con_ref.shape
    row = lax.broadcasted_iota(jnp.int32, (tail, levels), 0)
    placed = jnp.zeros((tail, levels), f32)
    for r in range(2 * blocks):
        placed = jnp.where(row == r, info_ref[r:r + 1, :], placed)
    for ref, sign in zip(side_refs, signs("lat")):
        at = jnp.where(sign > 0, lat_tile - rim, 0)
        for m in range(members):
            for i in range(0, lon_tile, 2):
                pair = [con_ref[m, pl.ds(pl.multiple_of(at + (i + k) * lat_tile, 8), rim), :] for k in range(2)]
                row_at = (m * lon_tile + i) * rim
                ref[row_at:row_at + 2 * rim, :] = jnp.concatenate(pair, axis=0).astype(bf16)
        ref[members * lon_tile * rim:, :] = placed.astype(bf16)
    for m in range(members):
        low_ref[m * cells:(m + 1) * cells, :] = con_ref[m].astype(bf16)


def pick_kernel(lat_tile, blocks, info_ref, ens_ref, out_ref):
    members, cells, levels = ens_ref.shape
    slots = out_ref.shape[0]
    lon_pos = to_rows(lane_row(info_ref, 0, blocks, slots))
    lat_pos = to_rows(lane_row(info_ref, blocks, blocks, slots))
    cell_of = lon_pos * float(lat_tile) + lat_pos
    chosen = (fiota((slots, cells), 1) == cell_of).astype(bf16)
    for m in range(members):
        out_ref[:, m * levels:(m + 1) * levels] = dot(chosen, ens_ref[m]).astype(bf16)


def prep_kernel(dims, taps_lon, taps_lat, info_ref, low_ref, *refs):
    lon_tile, lat_tile, rim, members, blocks = dims
    count = (len(refs) - 3) // 3
    sides, base_ref, rims = refs[:count], refs[count], refs[count + 1:]
    slots, levels = base_ref.shape[0], low_ref.shape[1]
    cells, edge, flank = lon_tile * lat_tile, rim * lat_tile, rim * lon_tile
    lon_pos = to_rows(lane_row(info_ref, 0, blocks, slots))
    lat_pos = to_rows(lane_row(info_ref, blocks, blocks, slots))
    lane = fiota((slots, 128), 1)
    lon_w = band(lane - lon_pos, taps_lon).astype(bf16)
    lat_w = band(lane + float(rim - lat_tile) - lat_pos, taps_lat).astype(bf16)
    lon_side = [jnp.where(s > 0, float(lon_tile), float(-rim)) for s in signs("lon")]
    sections = [(cells, 0.0, 0.0, lat_tile)] + [(edge, o, 0.0, lat_tile) for o in lon_side]
    for s in signs("lat")[:count]:
        sections += [(edge, o, s * float(lat_tile), lat_tile) for o in lon_side]
        sections.append((flank, 0.0, jnp.where(s > 0, float(lat_tile), float(-rim)), rim))
    lon_at, lat_at = [], []
    for size, lon_off, lat_off, width in sections:
        cell = fiota((1, -(-size // 128) * 128), 1)
        lon_of = jnp.floor((cell + 0.5) * (1.0 / width))
        lon_at.append(jnp.where(cell < size, lon_of + (lon_off + float(rim)), -1.0))
        lat_at.append(cell - lon_of * float(width) + (lat_off + float(lat_tile)))
    lon_at, lat_at = jnp.concatenate(lon_at, axis=1), jnp.concatenate(lat_at, axis=1)
    place = fiota((128, lon_at.shape[1]), 0)
    lon_e = dot(lon_w[:, 0:64], (place[0:64] == lon_at).astype(bf16))
    lat_e = dot(lat_w, (place == lat_at).astype(bf16))
    weight = (lon_e * lat_e).astype(bf16)
    ends = [0]
    for size, _, _, _ in sections:
        ends.append(ends[-1] + -(-size // 128) * 128)
    pieces = [weight[:, e:e + section[0]] for e, section in zip(ends, sections)]
    for m in range(members):
        part = dot(pieces[0], low_ref[m * cells:(m + 1) * cells, :])
        for t, side in enumerate(sides):
            part += dot(pieces[3 * t + 5], side[m * flank:(m + 1) * flank, :])
        base_ref[:, m * levels:(m + 1) * levels] = part
    kept = pieces[1:3]
    for t in range(count):
        kept += pieces[3 * t + 3:3 * t + 5]
    for ref, piece in zip(rims, kept):
        ref[...] = piece


def part_kernel(blocks, base_ref, own_ref, values_ref, scale_ref, *refs):
    out_ref = refs[-1]
    count = (len(refs) + 2) // 5
    tails, weights, halos = refs[:count - 1], refs[count - 1:3 * count - 2], refs[3 * count - 2:-1]
    n_slots, levels = values_ref.shape
    slots, wide = base_ref.shape
    members = wide // levels
    block = weights[0].shape[1]
    total = jnp.zeros((slots, levels), f32)
    for m in range(members):
        lanes = slice(m * levels, (m + 1) * levels)
        spread = base_ref[:, lanes]
        for w, h in zip(weights, halos):
            spread += dot(w[...], h[m * block:(m + 1) * block, :])
        total += spread * own_ref[:, lanes].astype(f32)
    out_ref[slots:, :] = jnp.zeros((out_ref.shape[0] - slots, levels), f32)
    at = slots
    for t in range(count):
        for ref in halos[2 * t:2 * t + 2] + tails[t:t + 1]:
            rows = ref[...] if ref.shape[0] == tail else ref[members * block:, :]
            out_ref[at:at + 2 * blocks, :] = rows.astype(f32)[0:2 * blocks]
            at += 2 * blocks
    at += 2 * blocks
    mem = lax.axis_index("mem")
    for r in range(blocks):
        out_ref[at + r:at + r + 1, :] = owner_lanes(scale_ref[...], mem * n_slots - r * levels, levels)
    out_ref[0:slots, :] = total
    mine = pl.ds(pl.multiple_of(mem * n_slots, n_slots), n_slots)
    out_ref[mine, :] = out_ref[mine, :] - values_ref[...]


def last_kernel(blocks, count, part_ref, own_ref, weight_ref, halo_ref, out_ref, sent_ref):
    slots, block = weight_ref.shape
    levels = part_ref.shape[1]
    members = own_ref.shape[1] // levels
    total = part_ref[0:slots, :]
    for m in range(members):
        lanes = slice(m * levels, (m + 1) * levels)
        total += dot(weight_ref[...], halo_ref[m * block:(m + 1) * block, :]) * own_ref[:, lanes].astype(f32)
    out_ref[0:slots, :] = total
    out_ref[slots:, :] = part_ref[slots:, :]
    at = slots + 2 * blocks * (3 * count - 2)
    out_ref[at:at + 2 * blocks, :] = halo_ref[members * block:, :].astype(f32)[0:2 * blocks]
    sent_ref[...] = out_ref[...].astype(bf16)


def resid_kernel(blocks, tiles, own_ref, *refs):
    terms, (resid_ref, send_ref, extra_ref) = refs[:-3], refs[-3:]
    slots, wide = send_ref.shape
    levels = resid_ref.shape[1]
    total = terms[0][...]
    for t in terms[1:]:
        total = total + t[...].astype(f32)
    extra_ref[...] = total[slots:]
    resid = to_rows(lane_row(extra_ref, 2 * blocks * (3 * tiles - 1), blocks, slots)) * total[0:slots]
    for m in range(wide // levels):
        lanes = slice(m * levels, (m + 1) * levels)
        send_ref[:, lanes] = (own_ref[:, lanes].astype(f32) * resid).astype(bf16)
    resid_ref[...] = resid


def weight_kernel(dims, taps_lon, taps_lat, info_ref, extra_ref, resid_ref, out_ref, mine_ref):
    lon_tile, lat_tile, blocks, tiles = dims
    slots, levels = resid_ref.shape
    n_slots = mine_ref.shape[0]
    mine_ref[...] = resid_ref[pl.ds(pl.multiple_of(lax.axis_index("mem") * n_slots, n_slots), n_slots), :]
    rim = taps_lon.shape[1] // 2
    lon_sign, lat_sign = signs("lon"), signs("lat")
    at = 0
    placed = []
    for t in range(tiles):
        shift = 0.0 if t == 0 else lat_sign[t - 1] * float(lat_tile)
        beside = []
        for side in range(2):
            beside.append((lane_row(extra_ref, at, blocks, slots) + lon_sign[side] * float(lon_tile), lane_row(extra_ref, at + blocks, blocks, slots)))
            at += 2 * blocks
        if t == 0:
            here = (lane_row(info_ref, 0, blocks, slots), lane_row(info_ref, blocks, blocks, slots))
        else:
            here = after
        if t + 1 < tiles:
            after = (lane_row(extra_ref, at, blocks, slots), lane_row(extra_ref, at + blocks, blocks, slots))
            at += 2 * blocks
        placed.append([(lon_at, lat_at + shift) for lon_at, lat_at in [here] + beside])
    lon_pos = [placed[t][k][0] for k in range(3) for t in range(tiles)]
    lat_pos = [placed[t][k][1] for k in range(3) for t in range(tiles)]
    lon_pos, lat_pos = jnp.concatenate(lon_pos, axis=1), jnp.concatenate(lat_pos, axis=1)
    tall = 32
    lon_w = band(fiota((tall, lon_pos.shape[1]), 0) + rim - lon_pos, taps_lon)
    lat_w = band(fiota((tall, lat_pos.shape[1]), 0) + rim - lat_pos, taps_lat)
    cells = lon_tile * lat_tile
    lon_of = fiota((lon_tile, lat_tile, tall), 0).reshape(cells, tall)
    lat_of = fiota((lon_tile, lat_tile, tall), 1).reshape(cells, tall)
    place = fiota((cells, tall), 1)
    lon_e = dot((place == lon_of).astype(bf16), lon_w.astype(bf16))
    lat_e = dot((place == lat_of).astype(bf16), lat_w.astype(bf16))
    out_ref[...] = (lon_e * lat_e).astype(bf16)


def begin_kernel(group, edge, weight_ref, con_ref, *refs):
    sets, out_hbm, rest_ref, all_ref, buf, sem = refs[:-5], refs[-5], refs[-4], refs[-3], refs[-2], refs[-1]
    members, cells, levels = con_ref.shape
    slots = sets[0].shape[0]
    for s, ref in enumerate(sets):
        all_ref[s * slots:(s + 1) * slots, :] = ref[...]
    depth = len(sets) * slots
    last = signs("lon")[1] > 0
    done = pl.ds(pl.multiple_of(jnp.where(last, 0, edge), 16), cells - edge)
    left = pl.ds(pl.multiple_of(jnp.where(last, cells - edge, 0), 16), edge)
    copies = []
    for m in range(0, members, group):
        back = dot(weight_ref[:, 0:depth], all_ref[:, m * levels:(m + group) * levels])
        for k in range(group):
            con = con_ref[m + k]
            buf[m + k] = con - descent * (con + back[:, k * levels:(k + 1) * levels])
            copies.append(pltpu.make_async_copy(buf.at[m + k, done], out_hbm.at[m + k, done], sem.at[m + k]))
            copies[-1].start()
    for m in range(members):
        rest_ref[m] = buf[m, left, :]
    for copy in copies:
        copy.wait()


def end_kernel(group, weight_ref, rest_ref, begun_hbm, *refs):
    sets, out_hbm, all_ref, buf, sem = refs[:-4], refs[-4], refs[-3], refs[-2], refs[-1]
    members, edge, levels = rest_ref.shape
    cells = weight_ref.shape[0]
    slots = sets[0].shape[0]
    for s, ref in enumerate(sets):
        all_ref[s * slots:(s + 1) * slots, :] = ref[...]
    begin = weight_ref.shape[1] - len(sets) * slots
    left = pl.ds(pl.multiple_of(jnp.where(signs("lon")[1] > 0, cells - edge, 0), 16), edge)
    weight = weight_ref[left, begin:]
    copies = []
    for m in range(0, members, group):
        back = dot(weight, all_ref[:, m * levels:(m + group) * levels])
        for k in range(group):
            buf[m + k] = rest_ref[m + k] - descent * back[:, k * levels:(k + 1) * levels]
            copies.append(pltpu.make_async_copy(buf.at[m + k], out_hbm.at[m + k, left], sem.at[m + k]))
            copies[-1].start()
    for copy in copies:
        copy.wait()


def shards(controls, ensemble, taps_lon, taps_lat, obs_columns, obs_count, obs_quality, obs_values):
    rim = taps_lon.shape[0] // 2
    members, lon_tile, lat_tile, levels = controls.shape
    n_slots = obs_columns.shape[-1]
    n_mem = lax.axis_size("mem")
    slots = n_slots * n_mem
    blocks = (slots + levels - 1) // levels
    cells = lon_tile * lat_tile
    edge = rim * lat_tile
    wide = members * levels
    lon_pairs = pairings(lax.axis_size("lon"), True)
    lat_pairs = pairings(lax.axis_size("lat"), False)
    vmem = pl.BlockSpec(memory_space=pltpu.VMEM)
    hbm = pl.BlockSpec(memory_space=pltpu.HBM)
    shape = jax.ShapeDtypeStruct
    taps_lon, taps_lat = taps_lon.reshape(1, -1), taps_lat.reshape(1, -1)
    flat = controls.reshape(members, cells, levels)

    flank = rim * lon_tile
    first = controls[:, :rim].reshape(members * edge, levels)
    last = controls[:, lon_tile - rim:].reshape(members * edge, levels)
    rim1, rim2, info = pl.pallas_call(
        functools.partial(start_kernel, (lat_tile, blocks)),
        out_shape=[shape((members * edge + tail, levels), bf16)] * 2 + [shape((up8(2 * blocks), levels), f32)],
        in_specs=[vmem] * 3, out_specs=[vmem] * 3, compiler_params=params(),
    )(first, last, obs_columns.reshape(1, n_slots))
    low, *sides = pl.pallas_call(
        functools.partial(low_kernel, (rim, lon_tile, lat_tile, blocks)),
        out_shape=[shape((members * cells, levels), bf16)] + [shape((members * flank + tail, levels), bf16)] * len(lat_pairs),
        in_specs=[vmem] * 2, out_specs=[vmem] * (1 + len(lat_pairs)), compiler_params=params(),
    )(flat, info)
    halos = [lax.ppermute(r, "lon", p) for r, p in zip((rim1, rim2), lon_pairs)]
    sides = [lax.ppermute(r, "lat", p) for r, p in zip(sides, lat_pairs)]
    n_tiles = 1 + len(lat_pairs)
    live = lax.broadcasted_iota(jnp.int32, (1, n_slots), 1) < obs_count[0]
    scale = jnp.where(live, 0.5 * obs_quality[0, 0].astype(f32), 0.0)
    info, scale = lax.optimization_barrier((info, scale))
    step = 1
    while step < n_mem:
        info = info + lax.ppermute(info, "mem", [(i, i ^ step) for i in range(n_mem)])
        step *= 2
    n_rims = 2 * n_tiles

    own = pl.pallas_call(
        functools.partial(pick_kernel, lat_tile, blocks),
        out_shape=shape((slots, wide), bf16),
        in_specs=[vmem] * 2, out_specs=vmem, compiler_params=params(),
    )(info, ensemble.reshape(members, cells, levels))
    base, *weights = pl.pallas_call(
        functools.partial(prep_kernel, (lon_tile, lat_tile, rim, members, blocks)),
        out_shape=[shape((slots, wide), f32)] + [shape((slots, edge), bf16)] * n_rims,
        in_specs=[vmem] * (3 + n_tiles), out_specs=[vmem] * (1 + n_rims), compiler_params=params(),
    )(taps_lon, taps_lat, info, low, *sides)

    halos[0], own = lax.optimization_barrier((halos[0], own))
    rims = list(halos)
    for p in lat_pairs:
        rims += [lax.ppermute(h, "lat", p) for h in halos]

    tall = slots + (2 * blocks * (3 * n_tiles - 1) + blocks + 15) // 16 * 16
    tails = [t[members * flank:] for t in sides]
    part = pl.pallas_call(
        functools.partial(part_kernel, blocks),
        out_shape=shape((tall, levels), f32),
        in_specs=[vmem] * (2 + len(tails) + 2 * len(rims)), out_specs=vmem, compiler_params=params(),
    )(base, own, obs_values.reshape(n_slots, levels), scale, *tails, *weights[:-1], *rims[:-1])
    mine, sent = pl.pallas_call(
        functools.partial(last_kernel, blocks, n_tiles),
        out_shape=[shape((tall, levels), f32), shape((tall, levels), bf16)],
        in_specs=[vmem] * 4, out_specs=[vmem] * 2, compiler_params=params(),
    )(part, own, weights[-1], rims[-1])
    terms = sum_terms(mine, sent, n_mem)

    resid, send, extra = pl.pallas_call(
        functools.partial(resid_kernel, blocks, n_tiles),
        out_shape=[shape((slots, levels), f32), shape((slots, wide), bf16), shape((tall - slots, levels), f32)],
        in_specs=[vmem] * (1 + len(terms)), out_specs=[vmem] * 3, compiler_params=params(),
    )(own, *terms)

    row = [send] + [lax.ppermute(send, "lon", p) for p in lon_pairs]
    count = len(row) * n_tiles
    weight, resid = pl.pallas_call(
        functools.partial(weight_kernel, (lon_tile, lat_tile, blocks, n_tiles)),
        out_shape=[shape((cells, count * slots), bf16), shape((n_slots, levels), f32)],
        in_specs=[vmem] * 5, out_specs=[vmem] * 2, compiler_params=params(),
    )(taps_lon, taps_lat, info, extra, resid)
    row[1], weight = lax.optimization_barrier((row[1], weight))
    around = []
    for r in row:
        around += [r] + [lax.ppermute(r, "lat", q) for q in lat_pairs]
    group = 2 if members % 2 == 0 else 1
    late = n_tiles
    begun, rest = pl.pallas_call(
        functools.partial(begin_kernel, group, edge),
        out_shape=[shape((members, cells, levels), f32), shape((members, edge, levels), f32)],
        in_specs=[vmem] * (2 + count - late), out_specs=[hbm, vmem],
        scratch_shapes=[
            pltpu.VMEM(((count - late) * slots, wide), bf16),
            pltpu.VMEM((members, cells, levels), f32),
            pltpu.SemaphoreType.DMA((members,)),
        ],
        compiler_params=params(),
    )(weight, flat, *around[:-late])
    new = pl.pallas_call(
        functools.partial(end_kernel, group),
        out_shape=shape((members, cells, levels), f32),
        in_specs=[vmem] * 2 + [hbm] + [vmem] * late, out_specs=hbm,
        scratch_shapes=[
            pltpu.VMEM((late * slots, wide), bf16),
            pltpu.VMEM((members, edge, levels), f32),
            pltpu.SemaphoreType.DMA((members,)),
        ],
        input_output_aliases={2: 0}, compiler_params=params(),
    )(weight, rest, begun, *around[-late:])
    return (new.reshape(controls.shape), resid[None, None, None])


def solution(mesh):
    placed = (
        P("mem", "lon", "lat", None),
        P("mem", "lon", "lat", None),
        P(),
        P(),
        P("lon", "lat", "mem", None),
        P("lon", "lat", "mem"),
        P("lon", "lat", "mem", None),
        P("lon", "lat", "mem", None, None),
    )
    return jax.shard_map(
        shards,
        mesh=mesh,
        in_specs=placed,
        out_specs=(P("mem", "lon", "lat", None), P("lon", "lat", "mem", None, None)),
        check_vma=False,
    )
```

```python
import functools

import jax
import jax.numpy as jnp
from jax import lax
from jax.experimental import pallas as pl
from jax.experimental.pallas import tpu as pltpu
from jax.sharding import PartitionSpec as P

descent = 0.5
f32 = jnp.float32
bf16 = jnp.bfloat16
tail = 16


def pairings(size, wraps):
    even = [(i, i ^ 1) for i in range(size)]
    odd = []
    for i in range(size):
        j = i + 1 if i % 2 else i - 1
        if wraps:
            j = j % size
        if 0 <= j < size:
            odd.append((i, j))
    return [even, odd] if odd else [even]


def sum_terms(x, count):
    if count <= 4:
        return [x] + [lax.ppermute(x, "mem", [(i, i ^ b) for i in range(count)]) for b in range(1, count)]
    step = 1
    while step < count:
        other = lax.ppermute(x, "mem", [(i, i ^ step) for i in range(count)])
        step *= 2
        if step < count:
            x = x + other
    return [x, other]


def up8(n):
    return (n + 7) // 8 * 8


def signs(axis):
    even = lax.axis_index(axis) % 2 == 0
    return [jnp.where(even, 1.0, -1.0).astype(f32), jnp.where(even, -1.0, 1.0).astype(f32)]


def fiota(shape, dim):
    return lax.broadcasted_iota(jnp.int32, shape, dim).astype(f32)


def diagonal(rows, lanes, shift=0.0):
    return fiota((rows, lanes), 0) + shift == fiota((rows, lanes), 1)


def to_rows(lanes):
    n = lanes.shape[1]
    return jnp.sum(jnp.where(diagonal(n, n), lanes, 0.0), axis=1, keepdims=True)


def to_lanes(rows):
    n = rows.shape[0]
    return jnp.sum(jnp.where(diagonal(n, n), rows, 0.0), axis=0, keepdims=True)


def owner_lanes(lanes, first, width):
    here = diagonal(lanes.shape[1], width, first.astype(f32))
    return jnp.sum(jnp.where(here, to_rows(lanes), 0.0), axis=0, keepdims=True)


def lane_row(ref, first, blocks, slots):
    if blocks == 1:
        return ref[first:first + 1, 0:slots]
    return jnp.concatenate([ref[first + r:first + r + 1, :] for r in range(blocks)], axis=1)[:, 0:slots]


def band(distance, taps_ref):
    taps = taps_ref[...].astype(bf16).astype(f32)
    out = jnp.zeros_like(distance)
    for k in range(taps.shape[1]):
        out = jnp.where(distance == float(k), taps[:, k:k + 1], out)
    return out


def dot(a, b):
    return jnp.dot(a, b, preferred_element_type=f32)


def params(mib=32):
    return pltpu.CompilerParams(vmem_limit_bytes=mib * 1024 * 1024)


def start_kernel(dims, first_ref, last_ref, col_ref, rim1_ref, rim2_ref, info_ref):
    lat_tile, blocks = dims
    edge, levels = first_ref.shape
    n_slots = col_ref.shape[1]
    mem = lax.axis_index("mem")
    column = col_ref[...].astype(f32)
    lon_pos = jnp.floor((column + 0.5) * (1.0 / lat_tile))
    lat_pos = column - lon_pos * float(lat_tile)
    info_ref[...] = jnp.zeros_like(info_ref)
    row = lax.broadcasted_iota(jnp.int32, (tail, levels), 0)
    placed = jnp.zeros((tail, levels), f32)
    for f, lanes in enumerate((lon_pos, lat_pos)):
        for r in range(blocks):
            moved = owner_lanes(lanes, mem * n_slots - r * levels, levels)
            info_ref[f * blocks + r:f * blocks + r + 1, :] = moved
            placed = jnp.where(row == f * blocks + r, moved, placed)
    even = lax.axis_index("lon") % 2 == 0

    @pl.when(even)
    def _():
        rim1_ref[0:edge, :] = last_ref[...].astype(bf16)
        rim2_ref[0:edge, :] = first_ref[...].astype(bf16)

    @pl.when(jnp.logical_not(even))
    def _():
        rim1_ref[0:edge, :] = first_ref[...].astype(bf16)
        rim2_ref[0:edge, :] = last_ref[...].astype(bf16)

    for ref in (rim1_ref, rim2_ref):
        ref[edge:, :] = placed.astype(bf16)


def low_kernel(dims, con_ref, info_ref, low_ref, *side_refs):
    rim, lon_tile, lat_tile, blocks = dims
    members, cells, levels = con_ref.shape
    row = lax.broadcasted_iota(jnp.int32, (tail, levels), 0)
    placed = jnp.zeros((tail, levels), f32)
    for r in range(2 * blocks):
        placed = jnp.where(row == r, info_ref[r:r + 1, :], placed)
    for ref, sign in zip(side_refs, signs("lat")):
        at = jnp.where(sign > 0, lat_tile - rim, 0)
        for m in range(members):
            for i in range(0, lon_tile, 2):
                pair = [con_ref[m, pl.ds(pl.multiple_of(at + (i + k) * lat_tile, 8), rim), :] for k in range(2)]
                row_at = (m * lon_tile + i) * rim
                ref[row_at:row_at + 2 * rim, :] = jnp.concatenate(pair, axis=0).astype(bf16)
        ref[members * lon_tile * rim:, :] = placed.astype(bf16)
    for m in range(members):
        low_ref[m * cells:(m + 1) * cells, :] = con_ref[m].astype(bf16)


def pick_kernel(lat_tile, blocks, info_ref, ens_ref, out_ref):
    members, cells, levels = ens_ref.shape
    slots = out_ref.shape[0]
    lon_pos = to_rows(lane_row(info_ref, 0, blocks, slots))
    lat_pos = to_rows(lane_row(info_ref, blocks, blocks, slots))
    cell_of = lon_pos * float(lat_tile) + lat_pos
    chosen = (fiota((slots, cells), 1) == cell_of).astype(bf16)
    for m in range(members):
        out_ref[:, m * levels:(m + 1) * levels] = dot(chosen, ens_ref[m]).astype(bf16)


def prep_kernel(dims, taps_lon, taps_lat, info_ref, low_ref, *refs):
    lon_tile, lat_tile, rim, members, blocks = dims
    count = (len(refs) - 3) // 3
    sides, base_ref, rims = refs[:count], refs[count], refs[count + 1:]
    slots, levels = base_ref.shape[0], low_ref.shape[1]
    cells, edge, flank = lon_tile * lat_tile, rim * lat_tile, rim * lon_tile
    lon_pos = to_rows(lane_row(info_ref, 0, blocks, slots))
    lat_pos = to_rows(lane_row(info_ref, blocks, blocks, slots))
    lane = fiota((slots, 128), 1)
    lon_w = band(lane - lon_pos, taps_lon).astype(bf16)
    lat_w = band(lane + float(rim - lat_tile) - lat_pos, taps_lat).astype(bf16)
    lon_side = [jnp.where(s > 0, float(lon_tile), float(-rim)) for s in signs("lon")]
    sections = [(cells, 0.0, 0.0, lat_tile)] + [(edge, o, 0.0, lat_tile) for o in lon_side]
    for s in signs("lat")[:count]:
        sections += [(edge, o, s * float(lat_tile), lat_tile) for o in lon_side]
        sections.append((flank, 0.0, jnp.where(s > 0, float(lat_tile), float(-rim)), rim))
    lon_at, lat_at = [], []
    for size, lon_off, lat_off, width in sections:
        cell = fiota((1, -(-size // 128) * 128), 1)
        lon_of = jnp.floor((cell + 0.5) * (1.0 / width))
        lon_at.append(jnp.where(cell < size, lon_of + (lon_off + float(rim)), -1.0))
        lat_at.append(cell - lon_of * float(width) + (lat_off + float(lat_tile)))
    lon_at, lat_at = jnp.concatenate(lon_at, axis=1), jnp.concatenate(lat_at, axis=1)
    place = fiota((128, lon_at.shape[1]), 0)
    lon_e = dot(lon_w[:, 0:64], (place[0:64] == lon_at).astype(bf16))
    lat_e = dot(lat_w, (place == lat_at).astype(bf16))
    weight = (lon_e * lat_e).astype(bf16)
    ends = [0]
    for size, _, _, _ in sections:
        ends.append(ends[-1] + -(-size // 128) * 128)
    pieces = [weight[:, e:e + section[0]] for e, section in zip(ends, sections)]
    for m in range(members):
        part = dot(pieces[0], low_ref[m * cells:(m + 1) * cells, :])
        for t, side in enumerate(sides):
            part += dot(pieces[3 * t + 5], side[m * flank:(m + 1) * flank, :])
        base_ref[:, m * levels:(m + 1) * levels] = part
    kept = pieces[1:3]
    for t in range(count):
        kept += pieces[3 * t + 3:3 * t + 5]
    for ref, piece in zip(rims, kept):
        ref[...] = piece


def part_kernel(blocks, base_ref, own_ref, values_ref, scale_ref, *refs):
    out_ref = refs[-1]
    count = (len(refs) + 2) // 5
    tails, weights, halos = refs[:count - 1], refs[count - 1:3 * count - 2], refs[3 * count - 2:-1]
    n_slots, levels = values_ref.shape
    slots, wide = base_ref.shape
    members = wide // levels
    block = weights[0].shape[1]
    total = jnp.zeros((slots, levels), f32)
    for m in range(members):
        lanes = slice(m * levels, (m + 1) * levels)
        spread = base_ref[:, lanes]
        for w, h in zip(weights, halos):
            spread += dot(w[...], h[m * block:(m + 1) * block, :])
        total += spread * own_ref[:, lanes].astype(f32)
    out_ref[slots:, :] = jnp.zeros((out_ref.shape[0] - slots, levels), f32)
    at = slots
    for t in range(count):
        for ref in halos[2 * t:2 * t + 2] + tails[t:t + 1]:
            rows = ref[...] if ref.shape[0] == tail else ref[members * block:, :]
            out_ref[at:at + 2 * blocks, :] = rows.astype(f32)[0:2 * blocks]
            at += 2 * blocks
    at += 2 * blocks
    mem = lax.axis_index("mem")
    for r in range(blocks):
        out_ref[at + r:at + r + 1, :] = owner_lanes(scale_ref[...], mem * n_slots - r * levels, levels)
    out_ref[0:slots, :] = total
    mine = pl.ds(pl.multiple_of(mem * n_slots, n_slots), n_slots)
    out_ref[mine, :] = out_ref[mine, :] - values_ref[...]


def last_kernel(blocks, count, part_ref, own_ref, weight_ref, halo_ref, out_ref):
    slots, block = weight_ref.shape
    levels = part_ref.shape[1]
    members = own_ref.shape[1] // levels
    total = part_ref[0:slots, :]
    for m in range(members):
        lanes = slice(m * levels, (m + 1) * levels)
        total += dot(weight_ref[...], halo_ref[m * block:(m + 1) * block, :]) * own_ref[:, lanes].astype(f32)
    out_ref[0:slots, :] = total
    out_ref[slots:, :] = part_ref[slots:, :]
    at = slots + 2 * blocks * (3 * count - 2)
    out_ref[at:at + 2 * blocks, :] = halo_ref[members * block:, :].astype(f32)[0:2 * blocks]


def resid_kernel(blocks, tiles, own_ref, *refs):
    terms, (resid_ref, send_ref, extra_ref) = refs[:-3], refs[-3:]
    slots, wide = send_ref.shape
    levels = resid_ref.shape[1]
    total = terms[0][...]
    for t in terms[1:]:
        total = total + t[...]
    extra_ref[...] = total[slots:]
    resid = to_rows(lane_row(extra_ref, 2 * blocks * (3 * tiles - 1), blocks, slots)) * total[0:slots]
    for m in range(wide // levels):
        lanes = slice(m * levels, (m + 1) * levels)
        send_ref[:, lanes] = (own_ref[:, lanes].astype(f32) * resid).astype(bf16)
    resid_ref[...] = resid


def weight_kernel(dims, taps_lon, taps_lat, info_ref, extra_ref, resid_ref, out_ref, mine_ref):
    lon_tile, lat_tile, blocks, tiles = dims
    slots, levels = resid_ref.shape
    n_slots = mine_ref.shape[0]
    mine_ref[...] = resid_ref[pl.ds(pl.multiple_of(lax.axis_index("mem") * n_slots, n_slots), n_slots), :]
    rim = taps_lon.shape[1] // 2
    lon_sign, lat_sign = signs("lon"), signs("lat")
    at = 0
    placed = []
    for t in range(tiles):
        shift = 0.0 if t == 0 else lat_sign[t - 1] * float(lat_tile)
        beside = []
        for side in range(2):
            beside.append((lane_row(extra_ref, at, blocks, slots) + lon_sign[side] * float(lon_tile), lane_row(extra_ref, at + blocks, blocks, slots)))
            at += 2 * blocks
        if t == 0:
            here = (lane_row(info_ref, 0, blocks, slots), lane_row(info_ref, blocks, blocks, slots))
        else:
            here = after
        if t + 1 < tiles:
            after = (lane_row(extra_ref, at, blocks, slots), lane_row(extra_ref, at + blocks, blocks, slots))
            at += 2 * blocks
        placed.append([(lon_at, lat_at + shift) for lon_at, lat_at in [here] + beside])
    lon_pos = [placed[t][k][0] for k in range(3) for t in range(tiles)]
    lat_pos = [placed[t][k][1] for k in range(3) for t in range(tiles)]
    lon_pos, lat_pos = jnp.concatenate(lon_pos, axis=1), jnp.concatenate(lat_pos, axis=1)
    tall = 32
    lon_w = band(fiota((tall, lon_pos.shape[1]), 0) + rim - lon_pos, taps_lon)
    lat_w = band(fiota((tall, lat_pos.shape[1]), 0) + rim - lat_pos, taps_lat)
    cells = lon_tile * lat_tile
    lon_of = fiota((lon_tile, lat_tile, tall), 0).reshape(cells, tall)
    lat_of = fiota((lon_tile, lat_tile, tall), 1).reshape(cells, tall)
    place = fiota((cells, tall), 1)
    lon_e = dot((place == lon_of).astype(bf16), lon_w.astype(bf16))
    lat_e = dot((place == lat_of).astype(bf16), lat_w.astype(bf16))
    out_ref[...] = (lon_e * lat_e).astype(bf16)


def begin_kernel(group, edge, weight_ref, con_ref, *refs):
    sets, out_hbm, rest_ref, all_ref, buf, sem = refs[:-5], refs[-5], refs[-4], refs[-3], refs[-2], refs[-1]
    members, cells, levels = con_ref.shape
    slots = sets[0].shape[0]
    for s, ref in enumerate(sets):
        all_ref[s * slots:(s + 1) * slots, :] = ref[...]
    depth = len(sets) * slots
    last = signs("lon")[1] > 0
    done = pl.ds(pl.multiple_of(jnp.where(last, 0, edge), 16), cells - edge)
    left = pl.ds(pl.multiple_of(jnp.where(last, cells - edge, 0), 16), edge)
    copies = []
    for m in range(0, members, group):
        back = dot(weight_ref[:, 0:depth], all_ref[:, m * levels:(m + group) * levels])
        for k in range(group):
            con = con_ref[m + k]
            buf[m + k] = con - descent * (con + back[:, k * levels:(k + 1) * levels])
            copies.append(pltpu.make_async_copy(buf.at[m + k, done], out_hbm.at[m + k, done], sem.at[m + k]))
            copies[-1].start()
    for m in range(members):
        rest_ref[m] = buf[m, left, :]
    for copy in copies:
        copy.wait()


def end_kernel(group, weight_ref, rest_ref, begun_hbm, *refs):
    sets, out_hbm, all_ref, buf, sem = refs[:-4], refs[-4], refs[-3], refs[-2], refs[-1]
    members, edge, levels = rest_ref.shape
    cells = weight_ref.shape[0]
    slots = sets[0].shape[0]
    for s, ref in enumerate(sets):
        all_ref[s * slots:(s + 1) * slots, :] = ref[...]
    begin = weight_ref.shape[1] - len(sets) * slots
    left = pl.ds(pl.multiple_of(jnp.where(signs("lon")[1] > 0, cells - edge, 0), 16), edge)
    weight = weight_ref[left, begin:]
    copies = []
    for m in range(0, members, group):
        back = dot(weight, all_ref[:, m * levels:(m + group) * levels])
        for k in range(group):
            buf[m + k] = rest_ref[m + k] - descent * back[:, k * levels:(k + 1) * levels]
            copies.append(pltpu.make_async_copy(buf.at[m + k], out_hbm.at[m + k, left], sem.at[m + k]))
            copies[-1].start()
    for copy in copies:
        copy.wait()


def shards(controls, ensemble, taps_lon, taps_lat, obs_columns, obs_count, obs_quality, obs_values):
    rim = taps_lon.shape[0] // 2
    members, lon_tile, lat_tile, levels = controls.shape
    n_slots = obs_columns.shape[-1]
    n_mem = lax.axis_size("mem")
    slots = n_slots * n_mem
    blocks = (slots + levels - 1) // levels
    cells = lon_tile * lat_tile
    edge = rim * lat_tile
    wide = members * levels
    lon_pairs = pairings(lax.axis_size("lon"), True)
    lat_pairs = pairings(lax.axis_size("lat"), False)
    vmem = pl.BlockSpec(memory_space=pltpu.VMEM)
    hbm = pl.BlockSpec(memory_space=pltpu.HBM)
    shape = jax.ShapeDtypeStruct
    taps_lon, taps_lat = taps_lon.reshape(1, -1), taps_lat.reshape(1, -1)
    flat = controls.reshape(members, cells, levels)

    flank = rim * lon_tile
    first = controls[:, :rim].reshape(members * edge, levels)
    last = controls[:, lon_tile - rim:].reshape(members * edge, levels)
    rim1, rim2, info = pl.pallas_call(
        functools.partial(start_kernel, (lat_tile, blocks)),
        out_shape=[shape((members * edge + tail, levels), bf16)] * 2 + [shape((up8(2 * blocks), levels), f32)],
        in_specs=[vmem] * 3, out_specs=[vmem] * 3, compiler_params=params(),
    )(first, last, obs_columns.reshape(1, n_slots))
    low, *sides = pl.pallas_call(
        functools.partial(low_kernel, (rim, lon_tile, lat_tile, blocks)),
        out_shape=[shape((members * cells, levels), bf16)] + [shape((members * flank + tail, levels), bf16)] * len(lat_pairs),
        in_specs=[vmem] * 2, out_specs=[vmem] * (1 + len(lat_pairs)), compiler_params=params(),
    )(flat, info)
    halos = [lax.ppermute(r, "lon", p) for r, p in zip((rim1, rim2), lon_pairs)]
    sides = [lax.ppermute(r, "lat", p) for r, p in zip(sides, lat_pairs)]
    n_tiles = 1 + len(lat_pairs)
    live = lax.broadcasted_iota(jnp.int32, (1, n_slots), 1) < obs_count[0]
    scale = jnp.where(live, 0.5 * obs_quality[0, 0].astype(f32), 0.0)
    info, scale = lax.optimization_barrier((info, scale))
    step = 1
    while step < n_mem:
        info = info + lax.ppermute(info, "mem", [(i, i ^ step) for i in range(n_mem)])
        step *= 2
    n_rims = 2 * n_tiles

    own = pl.pallas_call(
        functools.partial(pick_kernel, lat_tile, blocks),
        out_shape=shape((slots, wide), bf16),
        in_specs=[vmem] * 2, out_specs=vmem, compiler_params=params(),
    )(info, ensemble.reshape(members, cells, levels))
    base, *weights = pl.pallas_call(
        functools.partial(prep_kernel, (lon_tile, lat_tile, rim, members, blocks)),
        out_shape=[shape((slots, wide), f32)] + [shape((slots, edge), bf16)] * n_rims,
        in_specs=[vmem] * (3 + n_tiles), out_specs=[vmem] * (1 + n_rims), compiler_params=params(),
    )(taps_lon, taps_lat, info, low, *sides)

    halos[0], own = lax.optimization_barrier((halos[0], own))
    rims = list(halos)
    for p in lat_pairs:
        rims += [lax.ppermute(h, "lat", p) for h in halos]

    tall = slots + up8(2 * blocks * (3 * n_tiles - 1) + blocks)
    tails = [t[members * flank:] for t in sides]
    part = pl.pallas_call(
        functools.partial(part_kernel, blocks),
        out_shape=shape((tall, levels), f32),
        in_specs=[vmem] * (2 + len(tails) + 2 * len(rims)), out_specs=vmem, compiler_params=params(),
    )(base, own, obs_values.reshape(n_slots, levels), scale, *tails, *weights[:-1], *rims[:-1])
    mine = pl.pallas_call(
        functools.partial(last_kernel, blocks, n_tiles),
        out_shape=shape((tall, levels), f32),
        in_specs=[vmem] * 4, out_specs=vmem, compiler_params=params(),
    )(part, own, weights[-1], rims[-1])
    terms = sum_terms(mine, n_mem)

    resid, send, extra = pl.pallas_call(
        functools.partial(resid_kernel, blocks, n_tiles),
        out_shape=[shape((slots, levels), f32), shape((slots, wide), bf16), shape((tall - slots, levels), f32)],
        in_specs=[vmem] * (1 + len(terms)), out_specs=[vmem] * 3, compiler_params=params(),
    )(own, *terms)

    row = [send] + [lax.ppermute(send, "lon", p) for p in lon_pairs]
    count = len(row) * n_tiles
    weight, resid = pl.pallas_call(
        functools.partial(weight_kernel, (lon_tile, lat_tile, blocks, n_tiles)),
        out_shape=[shape((cells, count * slots), bf16), shape((n_slots, levels), f32)],
        in_specs=[vmem] * 5, out_specs=[vmem] * 2, compiler_params=params(),
    )(taps_lon, taps_lat, info, extra, resid)
    row[1], weight = lax.optimization_barrier((row[1], weight))
    around = []
    for r in row:
        around += [r] + [lax.ppermute(r, "lat", q) for q in lat_pairs]
    group = members
    late = n_tiles
    begun, rest = pl.pallas_call(
        functools.partial(begin_kernel, group, edge),
        out_shape=[shape((members, cells, levels), f32), shape((members, edge, levels), f32)],
        in_specs=[vmem] * (2 + count - late), out_specs=[hbm, vmem],
        scratch_shapes=[
            pltpu.VMEM(((count - late) * slots, wide), bf16),
            pltpu.VMEM((members, cells, levels), f32),
            pltpu.SemaphoreType.DMA((members,)),
        ],
        compiler_params=params(),
    )(weight, flat, *around[:-late])
    new = pl.pallas_call(
        functools.partial(end_kernel, group),
        out_shape=shape((members, cells, levels), f32),
        in_specs=[vmem] * 2 + [hbm] + [vmem] * late, out_specs=hbm,
        scratch_shapes=[
            pltpu.VMEM((late * slots, wide), bf16),
            pltpu.VMEM((members, edge, levels), f32),
            pltpu.SemaphoreType.DMA((members,)),
        ],
        input_output_aliases={2: 0}, compiler_params=params(),
    )(weight, rest, begun, *around[-late:])
    return (new.reshape(controls.shape), resid[None, None, None])


def solution(mesh):
    placed = (
        P("mem", "lon", "lat", None),
        P("mem", "lon", "lat", None),
        P(),
        P(),
        P("lon", "lat", "mem", None),
        P("lon", "lat", "mem"),
        P("lon", "lat", "mem", None),
        P("lon", "lat", "mem", None, None),
    )
    return jax.shard_map(
        shards,
        mesh=mesh,
        in_specs=placed,
        out_specs=(P("mem", "lon", "lat", None), P("lon", "lat", "mem", None, None)),
        check_vma=False,
    )
```
